32 devices in a mesh: seq: 4 (over z), head: 2 (over core), dp: 4 (over y, x).
Axes of the slice: x: 2, y: 2, z: 4, core: 2. Of those that a mesh axis runs over, the one named last changes fastest.
Arguments:
- series: bfloat16 [4, 2048, 768], P('dp', 'seq'), may hold values from -6 to 6
- norm_attn: float32 [768], replicated, may hold values from 0.1 to 1.9
- qkv_weight: bfloat16 [768, 3, 768], P(None, None, 'head'), may hold values from -0.21875 to 0.21875
- out_weight: bfloat16 [768, 768], P('head'), may hold values from -0.21875 to 0.21875
- norm_moe: float32 [768], replicated, may hold values from 0.1 to 1.9
- router_weight: bfloat16 [768, 16], replicated, may hold values from -0.21875 to 0.21875
- expert_ids: int32 [4, 2048, 1], P('dp', ('seq', 'head')), may hold values from 0 to 15; in each aligned block of 256 rows (0 to 255, 256 to 511, ..., all dimensions but the last counted through in order) at most 32 rows name the same one
- gate_weight: bfloat16 [16, 768, 3072], P(('seq', 'dp'), None, 'head'), may hold values from -0.21875 to 0.21875
- up_weight: bfloat16 [16, 768, 3072], P(('seq', 'dp'), None, 'head'), may hold values from -0.21875 to 0.21875
- down_weight: bfloat16 [16, 3072, 768], P(('seq', 'dp'), 'head'), may hold values from -0.109375 to 0.109375
Outputs:
- layer_out: bfloat16 [4, 2048, 768], P('dp', ('seq', 'head'))
The draws below stay inside these ranges and needn't reach their ends.
Inputs may be any that keep to these rules, and one draw needn't show every extreme that they name: `expert_ids`: among the rows of one device (aligned blocks of 256 positions, counted over series and positions in order) at most 32 name the same expert, and in every draw some expert is named by exactly 32 rows of some device.
All inputs are finite; a program needn't handle non-finite values.
Results may differ from the reference program's by a relative error of at most 0.0041.
Values may be sent and summed in bfloat16 or wider, within the bound.
A program may use at most 128 MiB of HBM per device.

```python
import math
import jax
import jax.numpy as jnp
import numpy as np
from jax import lax

D = 768
HEADS = 6
HD = 128
FF = 3072
BLOCK = 512
BATCH = 4
LEN = 2048
EXPERTS = 16
ROWS_DEV = 256
CAP = 32


def draw_series(key, part):
    first_key, second_key = jax.random.split(key, 2)
    segment_count = LEN // 128
    noise_part = jax.random.normal(first_key, (BATCH, LEN, D), jnp.float32)
    offsets = jax.random.normal(second_key, (BATCH, segment_count, D), jnp.float32)
    values = 0.7 * (noise_part + jnp.repeat(offsets, 128, axis=1))
    return jnp.clip(values, -6.0, 6.0).astype(jnp.bfloat16)


def steps_of(stream_key, extent, pieces, low, largest):
    level = 1.0
    for dim, parts in pieces:
        draws = jax.random.uniform(jax.random.fold_in(jax.random.fold_in(stream_key, 6), dim), (parts,), jnp.float32, low / len(pieces), largest / len(pieces))
        level = level * jnp.repeat(jnp.exp(draws), extent[dim] // parts).reshape((-1,) + (1,) * (len(extent) - 1 - dim))
    return level


def deal_out(rng, own, number, rows, count, top, most, skew):
    order = jax.random.permutation(rng, count)
    heavy_load, ordinary = portions_of(count, rows * top, most, skew, True), portions_of(count, rows * top, most, skew, False)
    places = jnp.arange(count)

    def named(tallies, offset_by):
        used = int((tallies > 0).sum())
        fixed = max(1, used // 4)
        passed = fixed + (places - fixed + offset_by * (used - fixed)) % max(1, count - fixed)
        return jnp.zeros((count,), jnp.int32).at[order[jnp.where(places < fixed, places, passed)]].set(jnp.asarray(tallies, jnp.int32))

    tallies = jnp.where(number % 4 == 0, named(heavy_load, number // 4), named(ordinary, number - number // 4 - 1))
    mixed = jax.random.permutation(jax.random.fold_in(own, 3), count)
    source_of, receiver = mixed[0:count // 2 * 2:2], mixed[1:count // 2 * 2:2]
    room = jnp.minimum(tallies[source_of] - 1, most - tallies[receiver]) // 2
    room = jnp.where((source_of == order[0]) | (receiver == order[0]) | (tallies[receiver] == 0), 0, jnp.maximum(room, 0))
    passed = jax.random.randint(jax.random.fold_in(own, 4), (count // 2,), 0, 1 << 20) % (room + 1)
    tallies = tallies.at[source_of].add(-passed).at[receiver].add(passed)
    items = jnp.searchsorted(jnp.cumsum(tallies), jnp.arange(rows * top), side="right").astype(jnp.int32)
    listing = items.reshape(top, rows).T
    listing = listing[jax.random.permutation(jax.random.fold_in(own, 1), rows)]
    offset_by = jax.random.randint(jax.random.fold_in(own, 2), (rows, 1), 0, top)
    return jnp.take_along_axis(listing, (jnp.arange(top)[None, :] + offset_by) % top, axis=1)


def portions_of(count, total, bound, lean, full):
    loads = [(1 << 20) // math.isqrt(rank ** lean) + 1 for rank in range(1, count + 1)]
    largest = bound if full else min(bound, max(-(-total // count), total * loads[0] // sum(loads)))
    least = 1 if total - largest >= count - 1 else 0
    given, rest = [largest] + [least] * (count - 1), total - largest - least * (count - 1)
    while rest > 0:
        free = [i for i in range(1, count) if given[i] < largest] or [i for i in range(1, count) if given[i] < bound]
        pool, left = sum([loads[i] for i in free]), rest
        for i in free:
            addition = min(bound - given[i], max(1, left * loads[i] // pool), rest)
            given[i] = given[i] + addition
            rest = rest - addition
    return np.array(given)


def gaussian(key, shape, spread, reach, pieces=(), held_as=jnp.bfloat16):
    result = jax.random.normal(key, shape, jnp.float32) * spread
    if len(pieces) > 0:
        result = steps_of(key, shape, pieces, -0.22, 0.18) * result
    return jnp.clip(result, min=-reach, max=reach).astype(held_as)


def setup_inputs(seed: int = 0) -> dict:
    streams_of = jax.random.split(jax.random.key(seed), 11)
    series = draw_series(jax.random.fold_in(streams_of[10], 71), 0)
    norm_attn = jnp.clip(1.0 + 0.18 * jax.random.normal(streams_of[1], (D,), jnp.float32), 0.1, 1.9)
    qkv_weight = gaussian(streams_of[2], (D, 3, HEADS * HD), D ** -0.5, 0.21875, ((2, 2),))
    out_weight = gaussian(streams_of[3], (HEADS * HD, D), (HEADS * HD) ** -0.5, 0.21875, ((0, 2),))
    norm_moe = jnp.clip(1.0 + 0.18 * jax.random.normal(streams_of[4], (D,), jnp.float32), 0.1, 1.9)
    router_weight = gaussian(streams_of[5], (D, EXPERTS), D ** -0.5, 0.21875)
    expert_ids_keys = jax.random.split(jax.random.fold_in(streams_of[6], 1), BATCH * LEN // ROWS_DEV)
    expert_ids_turns = jax.random.permutation(jax.random.fold_in(streams_of[6], 3), BATCH * LEN // ROWS_DEV)
    expert_ids = jax.vmap(lambda own, number: deal_out(jax.random.fold_in(streams_of[6], 2), own, number, ROWS_DEV, EXPERTS, 1, CAP, 2))(expert_ids_keys, expert_ids_turns).reshape((BATCH, LEN, 1))
    gate_weight = gaussian(streams_of[7], (EXPERTS, D, FF), D ** -0.5, 0.21875, ((0, 16), (2, 2)))
    up_weight = gaussian(streams_of[8], (EXPERTS, D, FF), D ** -0.5, 0.21875, ((0, 16), (2, 2)))
    down_weight = gaussian(streams_of[9], (EXPERTS, FF, D), FF ** -0.5, 0.109375, ((0, 16), (1, 2)))
    return dict(series=series, norm_attn=norm_attn, qkv_weight=qkv_weight, out_weight=out_weight, norm_moe=norm_moe, router_weight=router_weight, expert_ids=expert_ids, gate_weight=gate_weight, up_weight=up_weight, down_weight=down_weight)


NORM_EPS = 1e-06

def rms_scale(values, gain):
    values = values.astype(jnp.float32)
    return values * lax.rsqrt(lax.optimization_barrier(jnp.mean(values * values, axis=-1, keepdims=True)) + NORM_EPS) * gain

def attend_series(queries, key_rows, value_rows):
    block_count = LEN // BLOCK
    query_blocks = queries.reshape(block_count, BLOCK, HEADS, HD)
    key_blocks = key_rows.reshape(block_count, BLOCK, HEADS, HD)
    value_blocks = value_rows.reshape(block_count, BLOCK, HEADS, HD)
    causal = jnp.arange(BLOCK)[:, None] >= jnp.arange(BLOCK)[None, :]

    def block_step(kv_state, inputs):
        query_part, key_part, value_part = inputs
        query_f = query_part.astype(jnp.float32)
        key_f = key_part.astype(jnp.float32)
        value_f = value_part.astype(jnp.float32)
        scores = jnp.einsum('qhd,khd->hqk', query_f, key_f, precision=lax.Precision.HIGHEST)
        scores = jnp.where(causal[None], scores, 0.0)
        scores = lax.optimization_barrier(scores.astype(jnp.bfloat16)).astype(jnp.float32)
        inside = jnp.einsum('hqk,khd->qhd', scores, value_f, precision=lax.Precision.HIGHEST)
        carried = jnp.einsum('qhd,hde->qhe', query_f, kv_state, precision=lax.Precision.HIGHEST)
        kv_state = kv_state + jnp.einsum('khd,khe->hde', key_f, value_f, precision=lax.Precision.HIGHEST)
        return (kv_state, inside + carried)
    initial = jnp.zeros((HEADS, HD, HD), jnp.float32)
    _, mixed_heads = lax.scan(block_step, initial, (query_blocks, key_blocks, value_blocks))
    return mixed_heads.reshape(LEN, HEADS, HD)

def reference(series, norm_attn, qkv_weight, out_weight, norm_moe, router_weight, expert_ids, gate_weight, up_weight, down_weight):
    total_rows = BATCH * LEN
    normed_in = rms_scale(series, norm_attn).astype(jnp.bfloat16)
    projected = jnp.dot(normed_in.reshape(total_rows, D), qkv_weight.reshape(D, 3 * HEADS * HD), preferred_element_type=jnp.float32).astype(jnp.bfloat16)
    projected = projected.reshape(BATCH, LEN, 3, HEADS, HD)
    position_scale = (jnp.arange(LEN).astype(jnp.float32) + 1.0) * jnp.sqrt(jnp.float32(HD))

    def one_series(qkv_parts):
        mixed_heads = attend_series(qkv_parts[:, 0], qkv_parts[:, 1], qkv_parts[:, 2])
        return (mixed_heads / position_scale[:, None, None]).astype(jnp.bfloat16)
    heads_out = lax.map(one_series, projected)
    attention = jnp.dot(heads_out.reshape(total_rows, HEADS * HD), out_weight, preferred_element_type=jnp.float32)
    residual = series.reshape(total_rows, D).astype(jnp.float32) + attention
    normed_moe = rms_scale(residual, norm_moe).astype(jnp.bfloat16)
    route_ids = expert_ids.reshape(total_rows).astype(jnp.int32)
    logits = jnp.dot(normed_moe, router_weight, preferred_element_type=jnp.float32)
    gate_value = jax.nn.sigmoid(jnp.take_along_axis(logits, route_ids[:, None], axis=1))
    slot_most = total_rows // ROWS_DEV * CAP
    sort_order = jnp.argsort(route_ids, stable=True).astype(jnp.int32)
    counts = jnp.zeros((EXPERTS,), jnp.int32).at[route_ids].add(1).astype(jnp.int32)
    starts = (jnp.cumsum(counts) - counts).astype(jnp.int32)
    slots = jnp.arange(slot_most).astype(jnp.int32)

    def one_expert(expert_index):
        place = jnp.clip(starts[expert_index] + slots, 0, total_rows - 1).astype(jnp.int32)
        source = sort_order[place]
        picked_rows = normed_moe[source]
        gate_proj = jnp.dot(picked_rows, gate_weight[expert_index], preferred_element_type=jnp.float32)
        up_proj = jnp.dot(picked_rows, up_weight[expert_index], preferred_element_type=jnp.float32)
        hidden = (jax.nn.silu(gate_proj) * up_proj).astype(jnp.bfloat16)
        expert_out = jnp.dot(hidden, down_weight[expert_index], preferred_element_type=jnp.float32).astype(jnp.bfloat16)
        live_slot = slots < counts[expert_index]
        return (jnp.where(live_slot[:, None], expert_out, jnp.zeros_like(expert_out)), source)
    expert_outs, sources = lax.map(one_expert, jnp.arange(EXPERTS).astype(jnp.int32))
    routed = jnp.zeros((total_rows, D), jnp.float32).at[sources.reshape(-1)].add(expert_outs.reshape(-1, D).astype(jnp.float32))
    layer_out = (residual + gate_value * routed).astype(jnp.bfloat16)
    return layer_out.reshape(BATCH, LEN, D)
```

```python
import functools

import jax
import jax.numpy as jnp
from jax import lax
from jax.experimental import pallas as pl
from jax.experimental.pallas import tpu as pltpu
from jax.sharding import PartitionSpec as P

HD = 128
BLOCK = 512
NORM_EPS = 1e-06
MESH = pl.DeviceIdType.MESH
F32 = jnp.float32
BF16 = jnp.bfloat16


def rms_scale(values, gain):
    return values * lax.rsqrt(jnp.mean(values * values, axis=-1, keepdims=True) + NORM_EPS) * gain


def dot(a, b, dims=((1,), (0,))):
    return lax.dot_general(a, b, (dims, ((), ())), preferred_element_type=F32)


def layer_kernel(
    seq_n,
    dp_n,
    cap,
    series,
    norm_attn,
    qkv_weight,
    out_weight,
    norm_moe,
    router_weight,
    expert_ids,
    gate_hbm,
    up_hbm,
    down_hbm,
    layer_out,
    gate_v,
    up_v,
    down_v,
    normed,
    projected,
    state_own,
    state_in,
    before,
    inside,
    partial_out,
    partial_in,
    residual,
    routing,
    send_rows,
    recv_rows,
    out_rows,
    back_rows,
    own_sem,
    w_send,
    w_recv,
    s_send,
    s_recv,
    r_send,
    r_recv,
    d_send,
    d_recv,
    b_send,
    b_recv,
):
    z = lax.axis_index("seq")
    head = lax.axis_index("head")
    y = lax.axis_index("dp")
    other = 1 - head
    me = z * dp_n + y
    tokens, width = series.shape
    rows = tokens // 2
    local = qkv_weight.shape[1] // 3
    heads = local // HD
    half = rows

    def step_of(i):
        return (1 + (seq_n // 2 + i - 2 + seq_n - 1) % (seq_n - 1)) * ((i + seq_n - 1) // seq_n)

    def for_peers(i, sign, act):
        k = step_of(i)
        there = (z + sign * k + seq_n) % seq_n
        for d in range(dp_n):
            col = (y + sign * d + dp_n) % dp_n
            if d == 0:
                @pl.when(k != 0)
                def _():
                    act(there, col)
            else:
                act(there, col)
        return there

    def slab(expert):
        return pl.ds(pl.multiple_of(expert * cap, cap), cap)

    barrier = pltpu.get_barrier_semaphore()
    pl.semaphore_signal(barrier, inc=1, device_id={"head": other}, device_id_type=MESH)

    def greet(i, carry):
        for_peers(
            i,
            1,
            lambda a, b: pl.semaphore_signal(
                barrier, inc=1, device_id={"seq": a, "dp": b}, device_id_type=MESH
            ),
        )
        return carry

    lax.fori_loop(0, seq_n, greet, 0)

    weights = ((gate_hbm, gate_v), (up_hbm, up_v), (down_hbm, down_v))
    own_copies = [
        pltpu.make_async_copy(src.at[0], dst.at[0], own_sem.at[j])
        for j, (src, dst) in enumerate(weights)
    ]
    far_copies = [
        pltpu.make_async_remote_copy(
            src_ref=src.at[0],
            dst_ref=dst.at[1],
            send_sem=w_send.at[j],
            recv_sem=w_recv.at[j],
            device_id={"head": other},
            device_id_type=MESH,
        )
        for j, (src, dst) in enumerate(weights)
    ]
    for copy in own_copies:
        copy.start()

    normed[...] = rms_scale(series[...].astype(F32), norm_attn[...]).astype(BF16)
    projected[:, local:] = dot(normed[...], qkv_weight[:, local:]).astype(BF16)
    for h in range(heads):
        at = pl.ds(h * HD, HD)
        keys = projected[:, local + h * HD : local + (h + 1) * HD]
        values = projected[:, 2 * local + h * HD : 2 * local + (h + 1) * HD]
        state_own[at, :] = dot(keys, values, ((0,), (0,))).astype(BF16)

    pl.semaphore_wait(barrier, seq_n * dp_n)

    def state_copy(to):
        return pltpu.make_async_remote_copy(
            src_ref=state_own,
            dst_ref=state_in.at[z],
            send_sem=s_send.at[to],
            recv_sem=s_recv.at[z],
            device_id={"seq": to},
            device_id_type=MESH,
        )

    def send_state(j, carry):
        state_copy(seq_n - 1 - j).start()
        return carry

    lax.fori_loop(0, seq_n - 1 - z, send_state, 0)
    far_copies[0].start()
    far_copies[1].start()

    projected[:, :local] = dot(normed[...], qkv_weight[:, :local]).astype(BF16)
    for h in range(heads):
        cols = slice(h * HD, (h + 1) * HD)
        for part in range(2):
            low, high = part * half, (part + 1) * half
            q = projected[low:high, cols]
            keys = projected[:high, local + h * HD : local + (h + 1) * HD]
            values = projected[:high, 2 * local + h * HD : 2 * local + (h + 1) * HD]
            scores = dot(q, keys, ((1,), (1,)))
            t = lax.broadcasted_iota(jnp.int32, scores.shape, 0) + low
            s = lax.broadcasted_iota(jnp.int32, scores.shape, 1)
            scores = jnp.where(t >= s, scores, 0.0).astype(BF16)
            inside[low:high, cols] = dot(scores, values)

    ids = expert_ids[...]
    experts = router_weight.shape[1]
    picked = ids == lax.broadcasted_iota(jnp.int32, (rows, experts), 1)
    picked_f = picked.astype(F32)
    earlier = lax.broadcasted_iota(jnp.int32, (rows, rows), 1) < lax.broadcasted_iota(
        jnp.int32, (rows, rows), 0
    )
    ranks = dot(earlier.astype(F32).astype(BF16), picked_f.astype(BF16))
    rank = jnp.sum(ranks * picked_f, axis=1, keepdims=True)
    slot = ids * cap + rank.astype(jnp.int32)
    routing[...] = (
        (slot == lax.broadcasted_iota(jnp.int32, routing.shape, 1)).astype(F32).astype(BF16)
    )

    before[...] = jnp.zeros_like(before)

    def add_state(j, carry):
        pltpu.make_async_remote_copy(
            src_ref=state_own,
            dst_ref=state_in.at[j],
            send_sem=s_send.at[j],
            recv_sem=s_recv.at[j],
            device_id={"seq": j},
            device_id_type=MESH,
        ).wait_recv()
        before[...] += state_in[j].astype(F32)
        return carry

    lax.fori_loop(0, z, add_state, 0)

    state_hi = before[...].astype(BF16)
    state_lo = (before[...] - state_hi.astype(F32)).astype(BF16)

    def project_out(which):
        start = pl.multiple_of(which * half, half)
        at = pl.ds(start, half)
        position = z * tokens + start + 1 + lax.broadcasted_iota(jnp.int32, (half, 1), 0)
        scale = 1.0 / (position.astype(F32) * jnp.sqrt(F32(HD)))
        mixed = []
        for h in range(heads):
            cols = slice(h * HD, (h + 1) * HD)
            q = projected[at, cols]
            carried = dot(q, state_hi[cols]) + dot(q, state_lo[cols])
            mixed.append(((inside[at, cols] + carried) * scale).astype(BF16))
        return dot(jnp.concatenate(mixed, axis=1), out_weight[...])

    partial_out[...] = project_out(other)
    sum_copy = pltpu.make_async_remote_copy(
        src_ref=partial_out,
        dst_ref=partial_in,
        send_sem=r_send,
        recv_sem=r_recv,
        device_id={"head": other},
        device_id_type=MESH,
    )
    sum_copy.start()
    far_copies[2].start()
    own_at = pl.ds(pl.multiple_of(head * half, half), half)
    residual[...] = project_out(head) + series[own_at, :].astype(F32)
    sum_copy.wait_recv()
    total = residual[...] + partial_in[...]
    residual[...] = total
    normed_moe = rms_scale(total, norm_moe[...]).astype(BF16)
    send_rows[...] = dot(routing[...], normed_moe, ((0,), (0,))).astype(BF16)

    def row_copy(to_z, to_y):
        to = to_z * dp_n + to_y
        return pltpu.make_async_remote_copy(
            src_ref=send_rows.at[slab(to)],
            dst_ref=recv_rows.at[slab(me)],
            send_sem=d_send.at[to],
            recv_sem=d_recv.at[me],
            device_id={"seq": to_z, "dp": to_y},
            device_id_type=MESH,
        )

    def row_arrival(from_z, from_y):
        source = from_z * dp_n + from_y
        return pltpu.make_async_remote_copy(
            src_ref=send_rows.at[slab(source)],
            dst_ref=recv_rows.at[slab(source)],
            send_sem=d_send.at[source],
            recv_sem=d_recv.at[source],
            device_id={"seq": from_z, "dp": from_y},
            device_id_type=MESH,
        )

    def back_copy(to_z, to_y):
        to = to_z * dp_n + to_y
        return pltpu.make_async_remote_copy(
            src_ref=out_rows.at[slab(to)],
            dst_ref=back_rows.at[slab(me)],
            send_sem=b_send.at[to],
            recv_sem=b_recv.at[me],
            device_id={"seq": to_z, "dp": to_y},
            device_id_type=MESH,
        )

    def back_arrival(from_z, from_y):
        source = from_z * dp_n + from_y
        return pltpu.make_async_remote_copy(
            src_ref=out_rows.at[slab(source)],
            dst_ref=back_rows.at[slab(source)],
            send_sem=b_send.at[source],
            recv_sem=b_recv.at[source],
            device_id={"seq": from_z, "dp": from_y},
            device_id_type=MESH,
        )

    def dispatch(i, carry):
        for_peers(i, 1, lambda a, b: row_copy(a, b).start())
        return carry

    lax.fori_loop(0, seq_n, dispatch, 0)
    recv_rows[slab(me), :] = send_rows[slab(me), :]

    logits = dot(normed_moe, router_weight[...])
    gate_value = jax.nn.sigmoid(jnp.sum(logits * picked_f, axis=1, keepdims=True))

    for copy in own_copies:
        copy.wait()
    for copy in far_copies:
        copy.wait()

    group = dp_n * cap
    units = gate_v.shape[2]
    tile = units // 3

    def expert_group(i, carry):
        source_z = for_peers(i, -1, lambda a, b: row_arrival(a, b).wait_recv())
        at = pl.ds(pl.multiple_of(source_z * group, group), group)
        x = recv_rows[at, :]
        acc = jnp.zeros((group, width), F32)
        for side in range(2):
            for c in range(units // tile):
                cols = slice(c * tile, (c + 1) * tile)
                g = dot(x, gate_v[side, :, cols])
                u = dot(x, up_v[side, :, cols])
                hidden = (g * jax.nn.sigmoid(g) * u).astype(BF16)
                acc = acc + dot(hidden, down_v[side, cols, :])
        out_rows[at, :] = acc.astype(BF16)
        for_peers(i, -1, lambda a, b: back_copy(a, b).start())
        return carry

    lax.fori_loop(0, seq_n, expert_group, 0)
    back_rows[slab(me), :] = out_rows[slab(me), :]

    def await_back(i, carry):
        for_peers(i, 1, lambda a, b: back_arrival(a, b).wait_recv())
        return carry

    lax.fori_loop(0, seq_n, await_back, 0)
    routed = dot(routing[...], back_rows[...])
    layer_out[...] = (residual[...] + gate_value * routed).astype(BF16)

    def sent_rows(i, carry):
        for_peers(i, 1, lambda a, b: row_copy(a, b).wait_send())
        for_peers(i, -1, lambda a, b: back_copy(a, b).wait_send())
        return carry

    lax.fori_loop(0, seq_n, sent_rows, 0)

    def sent_state(j, carry):
        state_copy(seq_n - 1 - j).wait_send()
        return carry

    lax.fori_loop(0, seq_n - 1 - z, sent_state, 0)
    sum_copy.wait_send()


def on_device(
    series,
    norm_attn,
    qkv_weight,
    out_weight,
    norm_moe,
    router_weight,
    expert_ids,
    gate_weight,
    up_weight,
    down_weight,
):
    seq_n, head_n, dp_n = lax.axis_size("seq"), lax.axis_size("head"), lax.axis_size("dp")
    tokens, width = series.shape[1:]
    assert head_n == 2 and tokens == BLOCK and seq_n > 1
    rows = tokens // 2
    experts = router_weight.shape[1]
    peers = seq_n * dp_n
    assert experts == peers
    local = qkv_weight.shape[2]
    units = gate_weight.shape[2]
    capacity = 2 * rows // experts
    cap = -(-capacity // 16) * 16
    slots = experts * cap
    vmem = pl.BlockSpec(memory_space=pltpu.VMEM)
    hbm = pl.BlockSpec(memory_space=pl.ANY)
    dma = pltpu.SemaphoreType.DMA
    out = pl.pallas_call(
        functools.partial(layer_kernel, seq_n, dp_n, cap),
        out_shape=jax.ShapeDtypeStruct((rows, width), BF16),
        in_specs=[vmem] * 7 + [hbm] * 3,
        out_specs=vmem,
        scratch_shapes=[
            pltpu.VMEM((2, width, units), BF16),
            pltpu.VMEM((2, width, units), BF16),
            pltpu.VMEM((2, units, width), BF16),
            pltpu.VMEM((tokens, width), BF16),
            pltpu.VMEM((tokens, 3 * local), BF16),
            pltpu.VMEM((local, HD), BF16),
            pltpu.VMEM((seq_n, local, HD), BF16),
            pltpu.VMEM((local, HD), F32),
            pltpu.VMEM((tokens, local), F32),
            pltpu.VMEM((rows, width), F32),
            pltpu.VMEM((rows, width), F32),
            pltpu.VMEM((rows, width), F32),
            pltpu.VMEM((rows, slots), BF16),
            pltpu.VMEM((slots, width), BF16),
            pltpu.VMEM((slots, width), BF16),
            pltpu.VMEM((slots, width), BF16),
            pltpu.VMEM((slots, width), BF16),
            dma((3,)),
            dma((3,)),
            dma((3,)),
            dma((seq_n,)),
            dma((seq_n,)),
            dma,
            dma,
            dma((peers,)),
            dma((peers,)),
            dma((peers,)),
            dma((peers,)),
        ],
        compiler_params=pltpu.CompilerParams(
            collective_id=0, has_side_effects=True, vmem_limit_bytes=56 * 1024 * 1024
        ),
        name="layer",
    )(
        series[0],
        norm_attn[None],
        qkv_weight.reshape(width, 3 * local),
        out_weight,
        norm_moe[None],
        router_weight,
        expert_ids[0],
        gate_weight,
        up_weight,
        down_weight,
    )
    return out[None]


def solution(mesh):
    in_specs = (
        P("dp", "seq", None),
        P(),
        P(None, None, "head"),
        P("head", None),
        P(),
        P(),
        P("dp", ("seq", "head"), None),
        P(("seq", "dp"), None, "head"),
        P(("seq", "dp"), None, "head"),
        P(("seq", "dp"), "head", None),
    )
    out_specs = P("dp", ("seq", "head"), None)
    return jax.shard_map(
        on_device, mesh=mesh, in_specs=in_specs, out_specs=out_specs, check_vma=False
    )
```

```python
import functools

import jax
import jax.numpy as jnp
from jax import lax
from jax.experimental import pallas as pl
from jax.experimental.pallas import tpu as pltpu
from jax.sharding import PartitionSpec as P

HD = 128
BLOCK = 512
NORM_EPS = 1e-06
MESH = pl.DeviceIdType.MESH
F32 = jnp.float32
BF16 = jnp.bfloat16


def rms_scale(values, gain):
    return values * lax.rsqrt(jnp.mean(values * values, axis=-1, keepdims=True) + NORM_EPS) * gain


def dot(a, b, dims=((1,), (0,))):
    return lax.dot_general(a, b, (dims, ((), ())), preferred_element_type=F32)


def layer_kernel(
    seq_n,
    dp_n,
    cap,
    series,
    norm_attn,
    qkv_weight,
    out_weight,
    norm_moe,
    router_weight,
    expert_ids,
    gate_hbm,
    up_hbm,
    down_hbm,
    layer_out,
    gate_v,
    up_v,
    down_v,
    normed,
    projected,
    state_own,
    state_in,
    before,
    inside,
    partial_out,
    partial_in,
    residual,
    routing,
    placing,
    hidden,
    send_rows,
    recv_rows,
    out_rows,
    back_rows,
    own_sem,
    w_send,
    w_recv,
    s_send,
    s_recv,
    r_send,
    r_recv,
    d_send,
    d_recv,
    b_send,
    b_recv,
):
    z = lax.axis_index("seq")
    head = lax.axis_index("head")
    y = lax.axis_index("dp")
    other = 1 - head
    me = z * dp_n + y
    tokens, width = series.shape
    rows = tokens // 2
    local = qkv_weight.shape[2]
    heads = local // HD
    half = rows

    def step_of(i):
        return (1 + (seq_n // 2 + i - 2 + seq_n - 1) % (seq_n - 1)) * ((i + seq_n - 1) // seq_n)

    def for_peers(i, sign, act):
        k = step_of(i)
        there = (z + sign * k + seq_n) % seq_n
        for d in range(dp_n):
            col = (y + sign * d + dp_n) % dp_n
            if d == 0:
                @pl.when(k != 0)
                def _():
                    act(there, col)
            else:
                act(there, col)
        return there

    def slab(expert):
        return pl.ds(pl.multiple_of(expert * cap, cap), cap)

    barrier = pltpu.get_barrier_semaphore()
    pl.semaphore_signal(barrier, inc=1, device_id={"head": other}, device_id_type=MESH)

    def greet(i, carry):
        for_peers(
            i,
            1,
            lambda a, b: pl.semaphore_signal(
                barrier, inc=1, device_id={"seq": a, "dp": b}, device_id_type=MESH
            ),
        )
        return carry

    lax.fori_loop(0, seq_n, greet, 0)

    weights = ((gate_hbm, gate_v), (up_hbm, up_v), (down_hbm, down_v))
    own_copies = [
        pltpu.make_async_copy(src.at[0], dst.at[0], own_sem.at[j])
        for j, (src, dst) in enumerate(weights)
    ]
    far_copies = [
        pltpu.make_async_remote_copy(
            src_ref=src.at[0],
            dst_ref=dst.at[1],
            send_sem=w_send.at[j],
            recv_sem=w_recv.at[j],
            device_id={"head": other},
            device_id_type=MESH,
        )
        for j, (src, dst) in enumerate(weights)
    ]
    for copy in own_copies:
        copy.start()

    normed[...] = rms_scale(series[...].astype(F32), norm_attn[...][None]).astype(BF16)
    for j in (1, 2):
        projected[:, j * local : (j + 1) * local] = dot(normed[...], qkv_weight[j]).astype(BF16)
    for h in range(heads):
        at = pl.ds(h * HD, HD)
        keys = projected[:, local + h * HD : local + (h + 1) * HD]
        values = projected[:, 2 * local + h * HD : 2 * local + (h + 1) * HD]
        state_own[at, :] = dot(keys, values, ((0,), (0,))).astype(BF16)

    pl.semaphore_wait(barrier, seq_n * dp_n)

    def state_copy(to):
        return pltpu.make_async_remote_copy(
            src_ref=state_own,
            dst_ref=state_in.at[z],
            send_sem=s_send.at[to],
            recv_sem=s_recv.at[z],
            device_id={"seq": to},
            device_id_type=MESH,
        )

    def send_state(j, carry):
        state_copy(seq_n - 1 - j).start()
        return carry

    lax.fori_loop(0, seq_n - 1 - z, send_state, 0)
    far_copies[0].start()
    far_copies[1].start()

    projected[:, :local] = dot(normed[...], qkv_weight[0]).astype(BF16)
    for h in range(heads):
        cols = slice(h * HD, (h + 1) * HD)
        for part in range(2):
            low, high = part * half, (part + 1) * half
            q = projected[low:high, cols]
            keys = projected[:high, local + h * HD : local + (h + 1) * HD]
            values = projected[:high, 2 * local + h * HD : 2 * local + (h + 1) * HD]
            scores = dot(q, keys, ((1,), (1,)))
            t = lax.broadcasted_iota(jnp.int32, scores.shape, 0) + low
            s = lax.broadcasted_iota(jnp.int32, scores.shape, 1)
            scores = jnp.where(t >= s, scores, 0.0).astype(BF16)
            inside[low:high, cols] = dot(scores, values)

    ids = expert_ids[...]
    experts = router_weight.shape[0]
    slots = routing.shape[1]
    picked_row = (ids == lax.broadcasted_iota(jnp.int32, (experts, rows), 0)).astype(F32)
    earlier = lax.broadcasted_iota(jnp.int32, (rows, rows), 0) < lax.broadcasted_iota(
        jnp.int32, (rows, rows), 1
    )
    ranks = dot(picked_row.astype(BF16), earlier.astype(F32).astype(BF16))
    rank = jnp.sum(ranks * picked_row, axis=0, keepdims=True)
    slot = ids * cap + rank.astype(jnp.int32)
    placing[...] = (
        (slot == lax.broadcasted_iota(jnp.int32, (slots, rows), 0)).astype(F32).astype(BF16)
    )
    columns = jnp.transpose(jnp.broadcast_to(slot.astype(F32), (HD, rows)))
    slot_column = columns[:, :1].astype(jnp.int32)
    routing[...] = (
        (slot_column == lax.broadcasted_iota(jnp.int32, (rows, slots), 1)).astype(F32).astype(BF16)
    )
    picked = (
        slot_column // cap == lax.broadcasted_iota(jnp.int32, (rows, experts), 1)
    ).astype(F32)

    before[...] = jnp.zeros_like(before)

    def add_state(j, carry):
        pltpu.make_async_remote_copy(
            src_ref=state_own,
            dst_ref=state_in.at[j],
            send_sem=s_send.at[j],
            recv_sem=s_recv.at[j],
            device_id={"seq": j},
            device_id_type=MESH,
        ).wait_recv()
        before[...] += state_in[j].astype(F32)
        return carry

    lax.fori_loop(0, z, add_state, 0)

    state_hi = before[...].astype(BF16)
    state_lo = (before[...] - state_hi.astype(F32)).astype(BF16)

    def project_out(which):
        start = pl.multiple_of(which * half, half)
        at = pl.ds(start, half)
        position = z * tokens + start + 1 + lax.broadcasted_iota(jnp.int32, (half, 1), 0)
        scale = 1.0 / (position.astype(F32) * jnp.sqrt(F32(HD)))
        mixed = []
        for h in range(heads):
            cols = slice(h * HD, (h + 1) * HD)
            q = projected[at, cols]
            carried = dot(q, state_hi[cols]) + dot(q, state_lo[cols])
            mixed.append(((inside[at, cols] + carried) * scale).astype(BF16))
        return dot(jnp.concatenate(mixed, axis=1), out_weight[...])

    partial_out[...] = project_out(other)
    sum_copy = pltpu.make_async_remote_copy(
        src_ref=partial_out,
        dst_ref=partial_in,
        send_sem=r_send,
        recv_sem=r_recv,
        device_id={"head": other},
        device_id_type=MESH,
    )
    sum_copy.start()
    far_copies[2].start()
    own_at = pl.ds(pl.multiple_of(head * half, half), half)
    residual[...] = project_out(head) + series[own_at, :].astype(F32)
    sum_copy.wait_recv()
    total = residual[...] + partial_in[...]
    residual[...] = total
    normed_moe = rms_scale(total, norm_moe[...][None]).astype(BF16)
    send_rows[...] = dot(placing[...], normed_moe).astype(BF16)

    def row_copy(to_z, to_y):
        to = to_z * dp_n + to_y
        return pltpu.make_async_remote_copy(
            src_ref=send_rows.at[slab(to)],
            dst_ref=recv_rows.at[slab(me)],
            send_sem=d_send.at[to],
            recv_sem=d_recv.at[me],
            device_id={"seq": to_z, "dp": to_y},
            device_id_type=MESH,
        )

    def row_arrival(from_z, from_y):
        source = from_z * dp_n + from_y
        return pltpu.make_async_remote_copy(
            src_ref=send_rows.at[slab(source)],
            dst_ref=recv_rows.at[slab(source)],
            send_sem=d_send.at[source],
            recv_sem=d_recv.at[source],
            device_id={"seq": from_z, "dp": from_y},
            device_id_type=MESH,
        )

    def back_copy(to_z, to_y):
        to = to_z * dp_n + to_y
        return pltpu.make_async_remote_copy(
            src_ref=out_rows.at[slab(to)],
            dst_ref=back_rows.at[slab(me)],
            send_sem=b_send.at[to],
            recv_sem=b_recv.at[me],
            device_id={"seq": to_z, "dp": to_y},
            device_id_type=MESH,
        )

    def back_arrival(from_z, from_y):
        source = from_z * dp_n + from_y
        return pltpu.make_async_remote_copy(
            src_ref=out_rows.at[slab(source)],
            dst_ref=back_rows.at[slab(source)],
            send_sem=b_send.at[source],
            recv_sem=b_recv.at[source],
            device_id={"seq": from_z, "dp": from_y},
            device_id_type=MESH,
        )

    def dispatch(i, carry):
        for_peers(i, 1, lambda a, b: row_copy(a, b).start())
        return carry

    lax.fori_loop(0, seq_n, dispatch, 0)
    recv_rows[slab(me), :] = send_rows[slab(me), :]

    logits = dot(normed_moe, router_weight[...], ((1,), (1,)))
    gate_value = jax.nn.sigmoid(jnp.sum(logits * picked, axis=1, keepdims=True))

    for copy in own_copies:
        copy.wait()
    for copy in far_copies:
        copy.wait()

    group = dp_n * cap
    units = gate_v.shape[2]
    tile = units // 3

    def expert_groups(i, carry):
        places = []
        for j in range(2):
            source_z = for_peers(2 * i + j, -1, lambda a, b: row_arrival(a, b).wait_recv())
            places.append(pl.ds(pl.multiple_of(source_z * group, group), group))
        x = jnp.concatenate([recv_rows[at, :] for at in places], axis=0)
        for side in range(2):
            for c in range(units // tile):
                cols = slice(c * tile, (c + 1) * tile)
                g = dot(x, gate_v[side, :, cols])
                u = dot(x, up_v[side, :, cols])
                hidden[:, side * units + c * tile : side * units + (c + 1) * tile] = (
                    g * jax.nn.sigmoid(g) * u
                ).astype(BF16)
        out = dot(hidden[:, :units], down_v[0]) + dot(hidden[:, units:], down_v[1])
        for j, at in enumerate(places):
            out_rows[at, :] = out[j * group : (j + 1) * group].astype(BF16)
            for_peers(2 * i + j, -1, lambda a, b: back_copy(a, b).start())
        return carry

    lax.fori_loop(0, seq_n // 2, expert_groups, 0)
    back_rows[slab(me), :] = out_rows[slab(me), :]

    def await_back(i, carry):
        for_peers(i, 1, lambda a, b: back_arrival(a, b).wait_recv())
        return carry

    lax.fori_loop(0, seq_n, await_back, 0)
    routed = dot(routing[...], back_rows[...])
    layer_out[...] = (residual[...] + gate_value * routed).astype(BF16)

    def sent_rows(i, carry):
        for_peers(i, 1, lambda a, b: row_copy(a, b).wait_send())
        for_peers(i, -1, lambda a, b: back_copy(a, b).wait_send())
        return carry

    lax.fori_loop(0, seq_n, sent_rows, 0)

    def sent_state(j, carry):
        state_copy(seq_n - 1 - j).wait_send()
        return carry

    lax.fori_loop(0, seq_n - 1 - z, sent_state, 0)
    sum_copy.wait_send()


def on_device(
    series,
    norm_attn,
    qkv_weight,
    out_weight,
    norm_moe,
    router_weight,
    expert_ids,
    gate_weight,
    up_weight,
    down_weight,
):
    seq_n, head_n, dp_n = lax.axis_size("seq"), lax.axis_size("head"), lax.axis_size("dp")
    tokens, width = series.shape[1:]
    assert head_n == 2 and tokens == BLOCK and seq_n % 2 == 0
    rows = tokens // 2
    experts = router_weight.shape[1]
    peers = seq_n * dp_n
    assert experts == peers
    local = qkv_weight.shape[2]
    units = gate_weight.shape[2]
    capacity = 2 * rows // experts
    cap = -(-capacity // 16) * 16
    slots = experts * cap
    vmem = pl.BlockSpec(memory_space=pltpu.VMEM)
    hbm = pl.BlockSpec(memory_space=pl.ANY)
    dma = pltpu.SemaphoreType.DMA
    out = pl.pallas_call(
        functools.partial(layer_kernel, seq_n, dp_n, cap),
        out_shape=jax.ShapeDtypeStruct((rows, width), BF16),
        in_specs=[vmem] * 7 + [hbm] * 3,
        out_specs=vmem,
        scratch_shapes=[
            pltpu.VMEM((2, width, units), BF16),
            pltpu.VMEM((2, width, units), BF16),
            pltpu.VMEM((2, units, width), BF16),
            pltpu.VMEM((tokens, width), BF16),
            pltpu.VMEM((tokens, 3 * local), BF16),
            pltpu.VMEM((local, HD), BF16),
            pltpu.VMEM((seq_n, local, HD), BF16),
            pltpu.VMEM((local, HD), F32),
            pltpu.VMEM((tokens, local), F32),
            pltpu.VMEM((rows, width), F32),
            pltpu.VMEM((rows, width), F32),
            pltpu.VMEM((rows, width), F32),
            pltpu.VMEM((rows, slots), BF16),
            pltpu.VMEM((slots, rows), BF16),
            pltpu.VMEM((2 * dp_n * cap, 2 * units), BF16),
            pltpu.VMEM((slots, width), BF16),
            pltpu.VMEM((slots, width), BF16),
            pltpu.VMEM((slots, width), BF16),
            pltpu.VMEM((slots, width), BF16),
            dma((3,)),
            dma((3,)),
            dma((3,)),
            dma((seq_n,)),
            dma((seq_n,)),
            dma,
            dma,
            dma((peers,)),
            dma((peers,)),
            dma((peers,)),
            dma((peers,)),
        ],
        compiler_params=pltpu.CompilerParams(
            collective_id=0, has_side_effects=True, vmem_limit_bytes=56 * 1024 * 1024
        ),
        name="layer",
    )(
        series[0],
        norm_attn,
        jnp.transpose(qkv_weight, (1, 0, 2)),
        out_weight,
        norm_moe,
        router_weight.T,
        expert_ids.reshape(1, rows),
        gate_weight,
        up_weight,
        down_weight,
    )
    return out[None]


def solution(mesh):
    in_specs = (
        P("dp", "seq", None),
        P(),
        P(None, None, "head"),
        P("head", None),
        P(),
        P(),
        P("dp", ("seq", "head"), None),
        P(("seq", "dp"), None, "head"),
        P(("seq", "dp"), None, "head"),
        P(("seq", "dp"), "head", None),
    )
    out_specs = P("dp", ("seq", "head"), None)
    return jax.shard_map(
        on_device, mesh=mesh, in_specs=in_specs, out_specs=out_specs, check_vma=False
    )
```

```python
import functools

import jax
import jax.numpy as jnp
from jax import lax
from jax.experimental import pallas as pl
from jax.experimental.pallas import tpu as pltpu
from jax.sharding import PartitionSpec as P

HD = 128
BLOCK = 512
NORM_EPS = 1e-06
MESH = pl.DeviceIdType.MESH
F32 = jnp.float32
BF16 = jnp.bfloat16


def rms_scale(values, gain):
    return values * lax.rsqrt(jnp.mean(values * values, axis=-1, keepdims=True) + NORM_EPS) * gain


def dot(a, b, dims=((1,), (0,))):
    return lax.dot_general(a, b, (dims, ((), ())), preferred_element_type=F32)


def layer_kernel(
    seq_n,
    dp_n,
    cap,
    series,
    norm_attn,
    qkv_weight,
    out_weight,
    norm_moe,
    router_weight,
    expert_ids,
    gate_hbm,
    up_hbm,
    down_hbm,
    layer_out,
    gate_v,
    up_v,
    down_v,
    normed,
    projected,
    state_own,
    state_in,
    before,
    inside,
    mixed_out,
    mixed_in,
    out_far,
    residual,
    routing,
    placing,
    hidden,
    send_rows,
    recv_rows,
    out_rows,
    back_rows,
    own_sem,
    w_send,
    w_recv,
    s_send,
    s_recv,
    r_send,
    r_recv,
    d_send,
    d_recv,
    b_send,
    b_recv,
):
    z = lax.axis_index("seq")
    head = lax.axis_index("head")
    y = lax.axis_index("dp")
    other = 1 - head
    me = z * dp_n + y
    tokens, width = series.shape
    rows = tokens // 2
    local = qkv_weight.shape[2]
    heads = local // HD
    half = rows

    def step_of(i):
        return (1 + (seq_n // 2 + i - 2 + seq_n - 1) % (seq_n - 1)) * ((i + seq_n - 1) // seq_n)

    def for_peers(i, sign, act):
        k = step_of(i)
        there = (z + sign * k + seq_n) % seq_n
        for d in range(dp_n):
            col = (y + sign * d + dp_n) % dp_n
            if d == 0:
                @pl.when(k != 0)
                def _():
                    act(there, col)
            else:
                act(there, col)
        return there

    def slab(expert):
        return pl.ds(pl.multiple_of(expert * cap, cap), cap)

    barrier = pltpu.get_barrier_semaphore()
    pl.semaphore_signal(barrier, inc=1, device_id={"head": other}, device_id_type=MESH)

    def greet(i, carry):
        for_peers(
            i,
            1,
            lambda a, b: pl.semaphore_signal(
                barrier, inc=1, device_id={"seq": a, "dp": b}, device_id_type=MESH
            ),
        )
        return carry

    lax.fori_loop(0, seq_n, greet, 0)

    def core_copy(src, dst, j):
        return pltpu.make_async_remote_copy(
            src_ref=src,
            dst_ref=dst,
            send_sem=r_send.at[j],
            recv_sem=r_recv.at[j],
            device_id={"head": other},
            device_id_type=MESH,
        )

    weights = ((gate_hbm, gate_v), (up_hbm, up_v), (down_hbm, down_v))
    own_copies = [
        pltpu.make_async_copy(src.at[0], dst.at[0], own_sem.at[j])
        for j, (src, dst) in enumerate(weights)
    ]
    far_copies = [
        pltpu.make_async_remote_copy(
            src_ref=src.at[0],
            dst_ref=dst.at[1],
            send_sem=w_send.at[j],
            recv_sem=w_recv.at[j],
            device_id={"head": other},
            device_id_type=MESH,
        )
        for j, (src, dst) in enumerate(weights)
    ]
    for copy in own_copies:
        copy.start()

    normed[...] = rms_scale(series[...].astype(F32), norm_attn[...][None]).astype(BF16)
    for j in (1, 2):
        projected[:, j * local : (j + 1) * local] = dot(normed[...], qkv_weight[j]).astype(BF16)
    for h in range(heads):
        at = pl.ds(h * HD, HD)
        keys = projected[:, local + h * HD : local + (h + 1) * HD]
        values = projected[:, 2 * local + h * HD : 2 * local + (h + 1) * HD]
        state_own[at, :] = dot(keys, values, ((0,), (0,))).astype(BF16)

    pl.semaphore_wait(barrier, seq_n * dp_n)

    def state_copy(to):
        return pltpu.make_async_remote_copy(
            src_ref=state_own,
            dst_ref=state_in.at[z],
            send_sem=s_send.at[to],
            recv_sem=s_recv.at[z],
            device_id={"seq": to},
            device_id_type=MESH,
        )

    def send_state(j, carry):
        state_copy(seq_n - 1 - j).start()
        return carry

    lax.fori_loop(0, seq_n - 1 - z, send_state, 0)
    out_copy = core_copy(out_weight, out_far, 1)
    out_copy.start()
    far_copies[0].start()
    far_copies[1].start()

    projected[:, :local] = dot(normed[...], qkv_weight[0]).astype(BF16)
    for h in range(heads):
        cols = slice(h * HD, (h + 1) * HD)
        for part in range(2):
            low, high = part * half, (part + 1) * half
            q = projected[low:high, cols]
            keys = projected[:high, local + h * HD : local + (h + 1) * HD]
            values = projected[:high, 2 * local + h * HD : 2 * local + (h + 1) * HD]
            scores = dot(q, keys, ((1,), (1,)))
            t = lax.broadcasted_iota(jnp.int32, scores.shape, 0) + low
            s = lax.broadcasted_iota(jnp.int32, scores.shape, 1)
            scores = jnp.where(t >= s, scores, 0.0).astype(BF16)
            inside[low:high, cols] = dot(scores, values)

    ids = expert_ids[...]
    experts = router_weight.shape[0]
    slots = routing.shape[1]
    picked_row = (ids == lax.broadcasted_iota(jnp.int32, (experts, rows), 0)).astype(F32)
    earlier = lax.broadcasted_iota(jnp.int32, (rows, rows), 0) < lax.broadcasted_iota(
        jnp.int32, (rows, rows), 1
    )
    ranks = dot(picked_row.astype(BF16), earlier.astype(F32).astype(BF16))
    rank = jnp.sum(ranks * picked_row, axis=0, keepdims=True)
    slot = ids * cap + rank.astype(jnp.int32)
    placing[...] = (
        (slot == lax.broadcasted_iota(jnp.int32, (slots, rows), 0)).astype(F32).astype(BF16)
    )
    columns = jnp.transpose(jnp.broadcast_to(slot.astype(F32), (HD, rows)))
    slot_column = columns[:, :1].astype(jnp.int32)
    routing[...] = (
        (slot_column == lax.broadcasted_iota(jnp.int32, (rows, slots), 1)).astype(F32).astype(BF16)
    )
    picked = (
        slot_column // cap == lax.broadcasted_iota(jnp.int32, (rows, experts), 1)
    ).astype(F32)

    before[...] = jnp.zeros_like(before)

    def add_state(j, carry):
        pltpu.make_async_remote_copy(
            src_ref=state_own,
            dst_ref=state_in.at[j],
            send_sem=s_send.at[j],
            recv_sem=s_recv.at[j],
            device_id={"seq": j},
            device_id_type=MESH,
        ).wait_recv()
        before[...] += state_in[j].astype(F32)
        return carry

    lax.fori_loop(0, z, add_state, 0)

    state_hi = before[...].astype(BF16)
    state_lo = (before[...] - state_hi.astype(F32)).astype(BF16)

    def mix(which):
        start = pl.multiple_of(which * half, half)
        at = pl.ds(start, half)
        position = z * tokens + start + 1 + lax.broadcasted_iota(jnp.int32, (half, 1), 0)
        scale = 1.0 / (position.astype(F32) * jnp.sqrt(F32(HD)))
        mixed = []
        for h in range(heads):
            cols = slice(h * HD, (h + 1) * HD)
            q = projected[at, cols]
            carried = dot(q, state_hi[cols]) + dot(q, state_lo[cols])
            mixed.append(((inside[at, cols] + carried) * scale).astype(BF16))
        return jnp.concatenate(mixed, axis=1)

    mixed_out[...] = mix(other)
    mixed_copy = core_copy(mixed_out, mixed_in, 0)
    mixed_copy.start()
    far_copies[2].start()
    own_at = pl.ds(pl.multiple_of(head * half, half), half)
    residual[...] = dot(mix(head), out_weight[...]) + series[own_at, :].astype(F32)
    out_copy.wait_recv()
    mixed_copy.wait_recv()
    total = residual[...] + dot(mixed_in[...], out_far[...])
    residual[...] = total
    normed_moe = rms_scale(total, norm_moe[...][None]).astype(BF16)
    send_rows[...] = dot(placing[...], normed_moe).astype(BF16)

    def row_copy(to_z, to_y):
        to = to_z * dp_n + to_y
        return pltpu.make_async_remote_copy(
            src_ref=send_rows.at[slab(to)],
            dst_ref=recv_rows.at[slab(me)],
            send_sem=d_send.at[to],
            recv_sem=d_recv.at[me],
            device_id={"seq": to_z, "dp": to_y},
            device_id_type=MESH,
        )

    def row_arrival(from_z, from_y):
        source = from_z * dp_n + from_y
        return pltpu.make_async_remote_copy(
            src_ref=send_rows.at[slab(source)],
            dst_ref=recv_rows.at[slab(source)],
            send_sem=d_send.at[source],
            recv_sem=d_recv.at[source],
            device_id={"seq": from_z, "dp": from_y},
            device_id_type=MESH,
        )

    def back_copy(to_z, to_y):
        to = to_z * dp_n + to_y
        return pltpu.make_async_remote_copy(
            src_ref=out_rows.at[slab(to)],
            dst_ref=back_rows.at[slab(me)],
            send_sem=b_send.at[to],
            recv_sem=b_recv.at[me],
            device_id={"seq": to_z, "dp": to_y},
            device_id_type=MESH,
        )

    def back_arrival(from_z, from_y):
        source = from_z * dp_n + from_y
        return pltpu.make_async_remote_copy(
            src_ref=out_rows.at[slab(source)],
            dst_ref=back_rows.at[slab(source)],
            send_sem=b_send.at[source],
            recv_sem=b_recv.at[source],
            device_id={"seq": from_z, "dp": from_y},
            device_id_type=MESH,
        )

    def dispatch(i):
        for j in range(2):
            for_peers(2 * i + j, 1, lambda a, b: row_copy(a, b).start())

    dispatch(0)
    recv_rows[slab(me), :] = send_rows[slab(me), :]

    logits = dot(normed_moe, router_weight[...], ((1,), (1,)))
    gate_value = jax.nn.sigmoid(jnp.sum(logits * picked, axis=1, keepdims=True))

    for copy in own_copies:
        copy.wait()
    for copy in far_copies:
        copy.wait()

    group = dp_n * cap
    units = gate_v.shape[2]
    tile = units // 3

    def expert_groups(i, carry):
        for j in range(2):
            for_peers(2 * i + j, 1, lambda a, b: row_copy(a, b).wait_send())

        @pl.when(i + 1 < seq_n // 2)
        def _():
            dispatch(i + 1)

        places = []
        for j in range(2):
            source_z = for_peers(2 * i + j, -1, lambda a, b: row_arrival(a, b).wait_recv())
            places.append(pl.ds(pl.multiple_of(source_z * group, group), group))
        x = jnp.concatenate([recv_rows[at, :] for at in places], axis=0)
        for side in range(2):
            for c in range(units // tile):
                cols = slice(c * tile, (c + 1) * tile)
                g = dot(x, gate_v[side, :, cols])
                u = dot(x, up_v[side, :, cols])
                hidden[:, side * units + c * tile : side * units + (c + 1) * tile] = (
                    g * jax.nn.sigmoid(g) * u
                ).astype(BF16)
        out = dot(hidden[:, :units], down_v[0]) + dot(hidden[:, units:], down_v[1])
        for j, at in enumerate(places):
            out_rows[at, :] = out[j * group : (j + 1) * group].astype(BF16)
            for_peers(2 * i + j, -1, lambda a, b: back_copy(a, b).start())
        return carry

    lax.fori_loop(0, seq_n // 2, expert_groups, 0)
    back_rows[slab(me), :] = out_rows[slab(me), :]

    def await_back(i, carry):
        for_peers(i, 1, lambda a, b: back_arrival(a, b).wait_recv())
        return carry

    lax.fori_loop(0, seq_n, await_back, 0)
    routed = dot(routing[...], back_rows[...])
    layer_out[...] = (residual[...] + gate_value * routed).astype(BF16)

    def sent_rows(i, carry):
        for_peers(i, -1, lambda a, b: back_copy(a, b).wait_send())
        return carry

    lax.fori_loop(0, seq_n, sent_rows, 0)

    def sent_state(j, carry):
        state_copy(seq_n - 1 - j).wait_send()
        return carry

    lax.fori_loop(0, seq_n - 1 - z, sent_state, 0)
    mixed_copy.wait_send()
    out_copy.wait_send()


def on_device(
    series,
    norm_attn,
    qkv_weight,
    out_weight,
    norm_moe,
    router_weight,
    expert_ids,
    gate_weight,
    up_weight,
    down_weight,
):
    seq_n, head_n, dp_n = lax.axis_size("seq"), lax.axis_size("head"), lax.axis_size("dp")
    tokens, width = series.shape[1:]
    assert head_n == 2 and tokens == BLOCK and seq_n % 2 == 0
    rows = tokens // 2
    experts = router_weight.shape[1]
    peers = seq_n * dp_n
    assert experts == peers
    local = qkv_weight.shape[2]
    units = gate_weight.shape[2]
    capacity = 2 * rows // experts
    cap = -(-capacity // 16) * 16
    slots = experts * cap
    vmem = pl.BlockSpec(memory_space=pltpu.VMEM)
    hbm = pl.BlockSpec(memory_space=pl.ANY)
    dma = pltpu.SemaphoreType.DMA
    out = pl.pallas_call(
        functools.partial(layer_kernel, seq_n, dp_n, cap),
        out_shape=jax.ShapeDtypeStruct((rows, width), BF16),
        in_specs=[vmem] * 7 + [hbm] * 3,
        out_specs=vmem,
        scratch_shapes=[
            pltpu.VMEM((2, width, units), BF16),
            pltpu.VMEM((2, width, units), BF16),
            pltpu.VMEM((2, units, width), BF16),
            pltpu.VMEM((tokens, width), BF16),
            pltpu.VMEM((tokens, 3 * local), BF16),
            pltpu.VMEM((local, HD), BF16),
            pltpu.VMEM((seq_n, local, HD), BF16),
            pltpu.VMEM((local, HD), F32),
            pltpu.VMEM((tokens, local), F32),
            pltpu.VMEM((rows, local), BF16),
            pltpu.VMEM((rows, local), BF16),
            pltpu.VMEM((local, width), BF16),
            pltpu.VMEM((rows, width), F32),
            pltpu.VMEM((rows, slots), BF16),
            pltpu.VMEM((slots, rows), BF16),
            pltpu.VMEM((2 * dp_n * cap, 2 * units), BF16),
            pltpu.VMEM((slots, width), BF16),
            pltpu.VMEM((slots, width), BF16),
            pltpu.VMEM((slots, width), BF16),
            pltpu.VMEM((slots, width), BF16),
            dma((3,)),
            dma((3,)),
            dma((3,)),
            dma((seq_n,)),
            dma((seq_n,)),
            dma((2,)),
            dma((2,)),
            dma((peers,)),
            dma((peers,)),
            dma((peers,)),
            dma((peers,)),
        ],
        compiler_params=pltpu.CompilerParams(
            collective_id=0, has_side_effects=True, vmem_limit_bytes=44 * 1024 * 1024
        ),
        name="layer",
    )(
        series[0],
        norm_attn,
        jnp.transpose(qkv_weight, (1, 0, 2)),
        out_weight,
        norm_moe,
        router_weight.T,
        expert_ids.reshape(1, rows),
        gate_weight,
        up_weight,
        down_weight,
    )
    return out[None]


def solution(mesh):
    in_specs = (
        P("dp", "seq", None),
        P(),
        P(None, None, "head"),
        P("head", None),
        P(),
        P(),
        P("dp", ("seq", "head"), None),
        P(("seq", "dp"), None, "head"),
        P(("seq", "dp"), None, "head"),
        P(("seq", "dp"), "head", None),
    )
    out_specs = P("dp", ("seq", "head"), None)
    return jax.shard_map(
        on_device, mesh=mesh, in_specs=in_specs, out_specs=out_specs, check_vma=False
    )
```

```python
import functools

import jax
import jax.numpy as jnp
from jax import lax
from jax.experimental import pallas as pl
from jax.experimental.pallas import tpu as pltpu
from jax.sharding import PartitionSpec as P

HD = 128
BLOCK = 512
NORM_EPS = 1e-06
MESH = pl.DeviceIdType.MESH
F32 = jnp.float32
BF16 = jnp.bfloat16


def rms_scale(values, gain):
    return values * lax.rsqrt(jnp.mean(values * values, axis=-1, keepdims=True) + NORM_EPS) * gain


def dot(a, b, dims=((1,), (0,))):
    return lax.dot_general(a, b, (dims, ((), ())), preferred_element_type=F32)


def layer_kernel(
    seq_n,
    dp_n,
    cap,
    series_hbm,
    norm_attn_hbm,
    qkv_hbm,
    out_hbm,
    norm_moe_hbm,
    router_hbm,
    ids_hbm,
    gate_hbm,
    up_hbm,
    down_hbm,
    layer_out,
    series,
    norm_attn,
    qkv_weight,
    out_weight,
    norm_moe,
    router_weight,
    expert_ids,
    gate_v,
    up_v,
    down_v,
    normed,
    projected,
    state_own,
    state_in,
    before,
    inside,
    mixed_out,
    mixed_in,
    out_far,
    residual,
    routing,
    placing,
    hidden,
    send_rows,
    recv_rows,
    out_rows,
    back_rows,
    in_sem,
    own_sem,
    w_send,
    w_recv,
    s_send,
    s_recv,
    r_send,
    r_recv,
    d_send,
    d_recv,
    b_send,
    b_recv,
):
    z = lax.axis_index("seq")
    head = lax.axis_index("head")
    y = lax.axis_index("dp")
    other = 1 - head
    me = z * dp_n + y
    tokens, width = series.shape
    rows = tokens // 2
    local = qkv_weight.shape[2]
    heads = local // HD
    half = rows

    def step_of(i):
        return (1 + (seq_n // 2 + i - 2 + seq_n - 1) % (seq_n - 1)) * ((i + seq_n - 1) // seq_n)

    def for_peers(i, sign, act):
        k = step_of(i)
        there = (z + sign * k + seq_n) % seq_n
        for d in range(dp_n):
            col = (y + sign * d + dp_n) % dp_n
            if d == 0:
                @pl.when(k != 0)
                def _():
                    act(there, col)
            else:
                act(there, col)
        return there

    def slab(expert):
        return pl.ds(pl.multiple_of(expert * cap, cap), cap)

    fetches = [
        pltpu.make_async_copy(src, dst, in_sem.at[j])
        for j, (src, dst) in enumerate(
            (
                (series_hbm, series),
                (norm_attn_hbm, norm_attn),
                (qkv_hbm.at[1], qkv_weight.at[1]),
                (qkv_hbm.at[2], qkv_weight.at[2]),
                (qkv_hbm.at[0], qkv_weight.at[0]),
                (ids_hbm, expert_ids),
                (out_hbm, out_weight),
                (norm_moe_hbm, norm_moe),
                (router_hbm, router_weight),
            )
        )
    ]
    for fetch in fetches:
        fetch.start()

    barrier = pltpu.get_barrier_semaphore()
    pl.semaphore_signal(barrier, inc=1, device_id={"head": other}, device_id_type=MESH)

    def greet(i, carry):
        for_peers(
            i,
            1,
            lambda a, b: pl.semaphore_signal(
                barrier, inc=1, device_id={"seq": a, "dp": b}, device_id_type=MESH
            ),
        )
        return carry

    lax.fori_loop(0, seq_n, greet, 0)

    def core_copy(src, dst, j):
        return pltpu.make_async_remote_copy(
            src_ref=src,
            dst_ref=dst,
            send_sem=r_send.at[j],
            recv_sem=r_recv.at[j],
            device_id={"head": other},
            device_id_type=MESH,
        )

    weights = ((gate_hbm, gate_v), (up_hbm, up_v), (down_hbm, down_v))
    own_copies = [
        pltpu.make_async_copy(src.at[0], dst.at[0], own_sem.at[j])
        for j, (src, dst) in enumerate(weights)
    ]
    far_copies = [
        pltpu.make_async_remote_copy(
            src_ref=src.at[0],
            dst_ref=dst.at[1],
            send_sem=w_send.at[j],
            recv_sem=w_recv.at[j],
            device_id={"head": other},
            device_id_type=MESH,
        )
        for j, (src, dst) in enumerate(weights)
    ]
    fetches[0].wait()
    fetches[1].wait()
    normed[...] = rms_scale(series[...].astype(F32), norm_attn[...][None]).astype(BF16)
    for j in (1, 2):
        fetches[1 + j].wait()
        projected[:, j * local : (j + 1) * local] = dot(normed[...], qkv_weight[j]).astype(BF16)
    for h in range(heads):
        at = pl.ds(h * HD, HD)
        keys = projected[:, local + h * HD : local + (h + 1) * HD]
        values = projected[:, 2 * local + h * HD : 2 * local + (h + 1) * HD]
        state_own[at, :] = dot(keys, values, ((0,), (0,))).astype(BF16)

    pl.semaphore_wait(barrier, seq_n * dp_n)

    def state_copy(to):
        return pltpu.make_async_remote_copy(
            src_ref=state_own,
            dst_ref=state_in.at[z],
            send_sem=s_send.at[to],
            recv_sem=s_recv.at[z],
            device_id={"seq": to},
            device_id_type=MESH,
        )

    def send_state(j, carry):
        state_copy(seq_n - 1 - j).start()
        return carry

    lax.fori_loop(0, seq_n - 1 - z, send_state, 0)
    for fetch in fetches[4:]:
        fetch.wait()
    out_copy = core_copy(out_weight, out_far, 1)
    out_copy.start()
    for copy in own_copies:
        copy.start()
    far_copies[0].start()
    far_copies[1].start()

    projected[:, :local] = dot(normed[...], qkv_weight[0]).astype(BF16)
    for h in range(heads):
        cols = slice(h * HD, (h + 1) * HD)
        for part in range(2):
            low, high = part * half, (part + 1) * half
            q = projected[low:high, cols]
            keys = projected[:high, local + h * HD : local + (h + 1) * HD]
            values = projected[:high, 2 * local + h * HD : 2 * local + (h + 1) * HD]
            scores = dot(q, keys, ((1,), (1,)))
            t = lax.broadcasted_iota(jnp.int32, scores.shape, 0) + low
            s = lax.broadcasted_iota(jnp.int32, scores.shape, 1)
            scores = jnp.where(t >= s, scores, 0.0).astype(BF16)
            inside[low:high, cols] = dot(scores, values)

    ids = expert_ids[...]
    experts = router_weight.shape[0]
    slots = routing.shape[1]
    picked_row = (ids == lax.broadcasted_iota(jnp.int32, (experts, rows), 0)).astype(F32)
    earlier = lax.broadcasted_iota(jnp.int32, (rows, rows), 0) < lax.broadcasted_iota(
        jnp.int32, (rows, rows), 1
    )
    ranks = dot(picked_row.astype(BF16), earlier.astype(F32).astype(BF16))
    rank = jnp.sum(ranks * picked_row, axis=0, keepdims=True)
    slot = ids * cap + rank.astype(jnp.int32)
    placing[...] = (
        (slot == lax.broadcasted_iota(jnp.int32, (slots, rows), 0)).astype(F32).astype(BF16)
    )
    columns = jnp.transpose(jnp.broadcast_to(slot.astype(F32), (HD, rows)))
    slot_column = columns[:, :1].astype(jnp.int32)
    routing[...] = (
        (slot_column == lax.broadcasted_iota(jnp.int32, (rows, slots), 1)).astype(F32).astype(BF16)
    )
    picked = (
        slot_column // cap == lax.broadcasted_iota(jnp.int32, (rows, experts), 1)
    ).astype(F32)

    before[...] = jnp.zeros_like(before)

    def add_state(j, carry):
        pltpu.make_async_remote_copy(
            src_ref=state_own,
            dst_ref=state_in.at[j],
            send_sem=s_send.at[j],
            recv_sem=s_recv.at[j],
            device_id={"seq": j},
            device_id_type=MESH,
        ).wait_recv()
        before[...] += state_in[j].astype(F32)
        return carry

    lax.fori_loop(0, z, add_state, 0)

    state_hi = before[...].astype(BF16)
    state_lo = (before[...] - state_hi.astype(F32)).astype(BF16)

    def mix(which):
        start = pl.multiple_of(which * half, half)
        at = pl.ds(start, half)
        position = z * tokens + start + 1 + lax.broadcasted_iota(jnp.int32, (half, 1), 0)
        scale = 1.0 / (position.astype(F32) * jnp.sqrt(F32(HD)))
        mixed = []
        for h in range(heads):
            cols = slice(h * HD, (h + 1) * HD)
            q = projected[at, cols]
            carried = dot(q, state_hi[cols]) + dot(q, state_lo[cols])
            mixed.append(((inside[at, cols] + carried) * scale).astype(BF16))
        return jnp.concatenate(mixed, axis=1)

    mixed_out[...] = mix(other)
    mixed_copy = core_copy(mixed_out, mixed_in, 0)
    mixed_copy.start()
    far_copies[2].start()
    own_at = pl.ds(pl.multiple_of(head * half, half), half)
    residual[...] = dot(mix(head), out_weight[...]) + series[own_at, :].astype(F32)
    out_copy.wait_recv()
    mixed_copy.wait_recv()
    total = residual[...] + dot(mixed_in[...], out_far[...])
    residual[...] = total
    normed_moe = rms_scale(total, norm_moe[...][None]).astype(BF16)
    send_rows[...] = dot(placing[...], normed_moe).astype(BF16)

    def row_copy(to_z, to_y):
        to = to_z * dp_n + to_y
        return pltpu.make_async_remote_copy(
            src_ref=send_rows.at[slab(to)],
            dst_ref=recv_rows.at[slab(me)],
            send_sem=d_send.at[to],
            recv_sem=d_recv.at[me],
            device_id={"seq": to_z, "dp": to_y},
            device_id_type=MESH,
        )

    def row_arrival(from_z, from_y):
        source = from_z * dp_n + from_y
        return pltpu.make_async_remote_copy(
            src_ref=send_rows.at[slab(source)],
            dst_ref=recv_rows.at[slab(source)],
            send_sem=d_send.at[source],
            recv_sem=d_recv.at[source],
            device_id={"seq": from_z, "dp": from_y},
            device_id_type=MESH,
        )

    def back_copy(to_z, to_y):
        to = to_z * dp_n + to_y
        return pltpu.make_async_remote_copy(
            src_ref=out_rows.at[slab(to)],
            dst_ref=back_rows.at[slab(me)],
            send_sem=b_send.at[to],
            recv_sem=b_recv.at[me],
            device_id={"seq": to_z, "dp": to_y},
            device_id_type=MESH,
        )

    def back_arrival(from_z, from_y):
        source = from_z * dp_n + from_y
        return pltpu.make_async_remote_copy(
            src_ref=out_rows.at[slab(source)],
            dst_ref=back_rows.at[slab(source)],
            send_sem=b_send.at[source],
            recv_sem=b_recv.at[source],
            device_id={"seq": from_z, "dp": from_y},
            device_id_type=MESH,
        )

    def dispatch(i):
        for j in range(2):
            for_peers(2 * i + j, 1, lambda a, b: row_copy(a, b).start())

    dispatch(0)
    recv_rows[slab(me), :] = send_rows[slab(me), :]

    logits = dot(normed_moe, router_weight[...], ((1,), (1,)))
    gate_value = jax.nn.sigmoid(jnp.sum(logits * picked, axis=1, keepdims=True))

    for copy in own_copies:
        copy.wait()
    for copy in far_copies:
        copy.wait()

    group = dp_n * cap
    units = gate_v.shape[2]
    tile = units // 3

    def expert_groups(i, carry):
        for j in range(2):
            for_peers(2 * i + j, 1, lambda a, b: row_copy(a, b).wait_send())

        @pl.when(i + 1 < seq_n // 2)
        def _():
            dispatch(i + 1)

        places = []
        for j in range(2):
            source_z = for_peers(2 * i + j, -1, lambda a, b: row_arrival(a, b).wait_recv())
            places.append(pl.ds(pl.multiple_of(source_z * group, group), group))
        x = jnp.concatenate([recv_rows[at, :] for at in places], axis=0)
        for side in range(2):
            for c in range(units // tile):
                cols = slice(c * tile, (c + 1) * tile)
                g = dot(x, gate_v[side, :, cols])
                u = dot(x, up_v[side, :, cols])
                hidden[:, side * units + c * tile : side * units + (c + 1) * tile] = (
                    g * jax.nn.sigmoid(g) * u
                ).astype(BF16)
        out = dot(hidden[:, :units], down_v[0]) + dot(hidden[:, units:], down_v[1])
        for j, at in enumerate(places):
            out_rows[at, :] = out[j * group : (j + 1) * group].astype(BF16)
            for_peers(2 * i + j, -1, lambda a, b: back_copy(a, b).start())
        return carry

    lax.fori_loop(0, seq_n // 2, expert_groups, 0)
    back_rows[slab(me), :] = out_rows[slab(me), :]

    def await_back(i, carry):
        for_peers(i, 1, lambda a, b: back_arrival(a, b).wait_recv())
        return carry

    lax.fori_loop(0, seq_n, await_back, 0)
    routed = dot(routing[...], back_rows[...])
    layer_out[...] = (residual[...] + gate_value * routed).astype(BF16)

    def sent_rows(i, carry):
        for_peers(i, -1, lambda a, b: back_copy(a, b).wait_send())
        return carry

    lax.fori_loop(0, seq_n, sent_rows, 0)

    def sent_state(j, carry):
        state_copy(seq_n - 1 - j).wait_send()
        return carry

    lax.fori_loop(0, seq_n - 1 - z, sent_state, 0)
    mixed_copy.wait_send()
    out_copy.wait_send()


def on_device(
    series,
    norm_attn,
    qkv_weight,
    out_weight,
    norm_moe,
    router_weight,
    expert_ids,
    gate_weight,
    up_weight,
    down_weight,
):
    seq_n, head_n, dp_n = lax.axis_size("seq"), lax.axis_size("head"), lax.axis_size("dp")
    tokens, width = series.shape[1:]
    assert head_n == 2 and tokens == BLOCK and seq_n % 2 == 0
    rows = tokens // 2
    experts = router_weight.shape[1]
    peers = seq_n * dp_n
    assert experts == peers
    local = qkv_weight.shape[2]
    units = gate_weight.shape[2]
    capacity = 2 * rows // experts
    cap = -(-capacity // 16) * 16
    slots = experts * cap
    vmem = pl.BlockSpec(memory_space=pltpu.VMEM)
    hbm = pl.BlockSpec(memory_space=pltpu.HBM)
    dma = pltpu.SemaphoreType.DMA
    out = pl.pallas_call(
        functools.partial(layer_kernel, seq_n, dp_n, cap),
        out_shape=jax.ShapeDtypeStruct((rows, width), BF16),
        in_specs=[hbm] * 10,
        out_specs=vmem,
        scratch_shapes=[
            pltpu.VMEM((tokens, width), BF16),
            pltpu.VMEM((width,), F32),
            pltpu.VMEM((3, width, local), BF16),
            pltpu.VMEM((local, width), BF16),
            pltpu.VMEM((width,), F32),
            pltpu.VMEM((experts, width), BF16),
            pltpu.VMEM((1, rows), jnp.int32),
            pltpu.VMEM((2, width, units), BF16),
            pltpu.VMEM((2, width, units), BF16),
            pltpu.VMEM((2, units, width), BF16),
            pltpu.VMEM((tokens, width), BF16),
            pltpu.VMEM((tokens, 3 * local), BF16),
            pltpu.VMEM((local, HD), BF16),
            pltpu.VMEM((seq_n, local, HD), BF16),
            pltpu.VMEM((local, HD), F32),
            pltpu.VMEM((tokens, local), F32),
            pltpu.VMEM((rows, local), BF16),
            pltpu.VMEM((rows, local), BF16),
            pltpu.VMEM((local, width), BF16),
            pltpu.VMEM((rows, width), F32),
            pltpu.VMEM((rows, slots), BF16),
            pltpu.VMEM((slots, rows), BF16),
            pltpu.VMEM((2 * dp_n * cap, 2 * units), BF16),
            pltpu.VMEM((slots, width), BF16),
            pltpu.VMEM((slots, width), BF16),
            pltpu.VMEM((slots, width), BF16),
            pltpu.VMEM((slots, width), BF16),
            dma((9,)),
            dma((3,)),
            dma((3,)),
            dma((3,)),
            dma((seq_n,)),
            dma((seq_n,)),
            dma((2,)),
            dma((2,)),
            dma((peers,)),
            dma((peers,)),
            dma((peers,)),
            dma((peers,)),
        ],
        compiler_params=pltpu.CompilerParams(
            collective_id=0, has_side_effects=True, vmem_limit_bytes=44 * 1024 * 1024
        ),
        name="layer",
    )(
        *[
            pltpu.with_memory_space_constraint(operand, pltpu.HBM)
            for operand in (
                series[0],
                norm_attn,
                jnp.transpose(qkv_weight, (1, 0, 2)),
                out_weight,
                norm_moe,
                router_weight.T,
                expert_ids.reshape(1, rows),
                gate_weight,
                up_weight,
                down_weight,
            )
        ]
    )
    return out[None]


def solution(mesh):
    in_specs = (
        P("dp", "seq", None),
        P(),
        P(None, None, "head"),
        P("head", None),
        P(),
        P(),
        P("dp", ("seq", "head"), None),
        P(("seq", "dp"), None, "head"),
        P(("seq", "dp"), None, "head"),
        P(("seq", "dp"), "head", None),
    )
    out_specs = P("dp", ("seq", "head"), None)
    return jax.shard_map(
        on_device, mesh=mesh, in_specs=in_specs, out_specs=out_specs, check_vma=False
    )
```

```python
import functools

import jax
import jax.numpy as jnp
from jax import lax
from jax.experimental import pallas as pl
from jax.experimental.pallas import tpu as pltpu
from jax.sharding import PartitionSpec as P

HD = 128
BLOCK = 512
NORM_EPS = 1e-06
MESH = pl.DeviceIdType.MESH
F32 = jnp.float32
BF16 = jnp.bfloat16


def rms_scale(values, gain):
    return values * lax.rsqrt(jnp.mean(values * values, axis=-1, keepdims=True) + NORM_EPS) * gain


def dot(a, b, dims=((1,), (0,))):
    return lax.dot_general(a, b, (dims, ((), ())), preferred_element_type=F32)


def layer_kernel(
    seq_n,
    dp_n,
    cap,
    series_hbm,
    norm_attn_hbm,
    qkv_hbm,
    out_hbm,
    norm_moe_hbm,
    router_hbm,
    ids_hbm,
    gate_hbm,
    up_hbm,
    down_hbm,
    layer_out,
    series,
    norm_attn,
    qkv_weight,
    out_weight,
    norm_moe,
    router_weight,
    expert_ids,
    gate_v,
    up_v,
    down_v,
    normed,
    projected,
    state_own,
    state_in,
    before,
    inside,
    mixed_out,
    mixed_in,
    out_far,
    residual,
    routing,
    placing,
    hidden,
    send_rows,
    recv_rows,
    out_rows,
    back_rows,
    in_sem,
    own_sem,
    w_send,
    w_recv,
    s_send,
    s_recv,
    r_send,
    r_recv,
    d_send,
    d_recv,
    b_send,
    b_recv,
):
    z = lax.axis_index("seq")
    head = lax.axis_index("head")
    y = lax.axis_index("dp")
    other = 1 - head
    me = z * dp_n + y
    tokens, width = series.shape
    rows = tokens // 2
    local = qkv_weight.shape[2]
    heads = local // HD
    half = rows

    def step_of(i):
        return (1 + (seq_n // 2 + i - 2 + seq_n - 1) % (seq_n - 1)) * ((i + seq_n - 1) // seq_n)

    def for_peers(i, sign, act):
        k = step_of(i)
        there = (z + sign * k + seq_n) % seq_n
        for d in range(dp_n):
            col = (y + sign * d + dp_n) % dp_n
            if d == 0:
                @pl.when(k != 0)
                def _():
                    act(there, col)
            else:
                act(there, col)
        return there

    def slab(expert):
        return pl.ds(pl.multiple_of(expert * cap, cap), cap)

    fetches = [
        pltpu.make_async_copy(src, dst, in_sem.at[j])
        for j, (src, dst) in enumerate(
            (
                (series_hbm, series),
                (norm_attn_hbm, norm_attn),
                (qkv_hbm.at[1], qkv_weight.at[1]),
                (qkv_hbm.at[2], qkv_weight.at[2]),
                (qkv_hbm.at[0], qkv_weight.at[0]),
                (ids_hbm, expert_ids),
                (out_hbm, out_weight),
                (norm_moe_hbm, norm_moe),
                (router_hbm, router_weight),
            )
        )
    ]
    for fetch in fetches:
        fetch.start()

    barrier = pltpu.get_barrier_semaphore()
    pl.semaphore_signal(barrier, inc=1, device_id={"head": other}, device_id_type=MESH)

    def greet(i, carry):
        for_peers(
            i,
            1,
            lambda a, b: pl.semaphore_signal(
                barrier, inc=1, device_id={"seq": a, "dp": b}, device_id_type=MESH
            ),
        )
        return carry

    lax.fori_loop(0, seq_n, greet, 0)

    def core_copy(src, dst, j):
        return pltpu.make_async_remote_copy(
            src_ref=src,
            dst_ref=dst,
            send_sem=r_send.at[j],
            recv_sem=r_recv.at[j],
            device_id={"head": other},
            device_id_type=MESH,
        )

    weights = ((gate_hbm, gate_v), (up_hbm, up_v), (down_hbm, down_v))
    own_copies = [
        pltpu.make_async_copy(src.at[0], dst.at[0], own_sem.at[j])
        for j, (src, dst) in enumerate(weights)
    ]
    far_copies = [
        pltpu.make_async_remote_copy(
            src_ref=src.at[0],
            dst_ref=dst.at[1],
            send_sem=w_send.at[j],
            recv_sem=w_recv.at[j],
            device_id={"head": other},
            device_id_type=MESH,
        )
        for j, (src, dst) in enumerate(weights)
    ]
    fetches[0].wait()
    fetches[1].wait()
    normed[...] = rms_scale(series[...].astype(F32), norm_attn[...][None]).astype(BF16)
    for j in (1, 2):
        fetches[1 + j].wait()
        projected[:, j * local : (j + 1) * local] = dot(normed[...], qkv_weight[j]).astype(BF16)
    for h in range(heads):
        at = pl.ds(h * HD, HD)
        keys = projected[:, local + h * HD : local + (h + 1) * HD]
        values = projected[:, 2 * local + h * HD : 2 * local + (h + 1) * HD]
        state_own[at, :] = dot(keys, values, ((0,), (0,))).astype(BF16)

    pl.semaphore_wait(barrier, seq_n * dp_n)

    def state_copy(to):
        return pltpu.make_async_remote_copy(
            src_ref=state_own,
            dst_ref=state_in.at[z],
            send_sem=s_send.at[to],
            recv_sem=s_recv.at[z],
            device_id={"seq": to},
            device_id_type=MESH,
        )

    def send_state(j, carry):
        state_copy(seq_n - 1 - j).start()
        return carry

    lax.fori_loop(0, seq_n - 1 - z, send_state, 0)
    for fetch in fetches[4:]:
        fetch.wait()
    out_copy = core_copy(out_weight, out_far, 1)
    out_copy.start()
    for copy in own_copies:
        copy.start()
    far_copies[0].start()
    far_copies[1].start()

    projected[:, :local] = dot(normed[...], qkv_weight[0]).astype(BF16)
    for h in range(heads):
        cols = slice(h * HD, (h + 1) * HD)
        for part in range(2):
            low, high = part * half, (part + 1) * half
            q = projected[low:high, cols]
            keys = projected[:high, local + h * HD : local + (h + 1) * HD]
            values = projected[:high, 2 * local + h * HD : 2 * local + (h + 1) * HD]
            scores = dot(q, keys, ((1,), (1,)))
            t = lax.broadcasted_iota(jnp.int32, scores.shape, 0) + low
            s = lax.broadcasted_iota(jnp.int32, scores.shape, 1)
            scores = jnp.where(t >= s, scores, 0.0).astype(BF16)
            inside[low:high, cols] = dot(scores, values)

    ids = expert_ids[...]
    experts = router_weight.shape[0]
    slots = routing.shape[1]
    picked_row = (ids == lax.broadcasted_iota(jnp.int32, (experts, rows), 0)).astype(F32)
    earlier = lax.broadcasted_iota(jnp.int32, (rows, rows), 0) < lax.broadcasted_iota(
        jnp.int32, (rows, rows), 1
    )
    ranks = dot(picked_row.astype(BF16), earlier.astype(F32).astype(BF16))
    rank = jnp.sum(ranks * picked_row, axis=0, keepdims=True)
    slot = ids * cap + rank.astype(jnp.int32)
    placing[...] = (
        (slot == lax.broadcasted_iota(jnp.int32, (slots, rows), 0)).astype(F32).astype(BF16)
    )
    columns = jnp.transpose(jnp.broadcast_to(slot.astype(F32), (HD, rows)))
    slot_column = columns[:, :1].astype(jnp.int32)
    routing[...] = (
        (slot_column == lax.broadcasted_iota(jnp.int32, (rows, slots), 1)).astype(F32).astype(BF16)
    )
    picked = (
        slot_column // cap == lax.broadcasted_iota(jnp.int32, (rows, experts), 1)
    ).astype(F32)

    before[...] = jnp.zeros_like(before)

    def add_state(j, carry):
        pltpu.make_async_remote_copy(
            src_ref=state_own,
            dst_ref=state_in.at[j],
            send_sem=s_send.at[j],
            recv_sem=s_recv.at[j],
            device_id={"seq": j},
            device_id_type=MESH,
        ).wait_recv()
        before[...] += state_in[j].astype(F32)
        return carry

    lax.fori_loop(0, z, add_state, 0)

    state_hi = before[...].astype(BF16)
    state_lo = (before[...] - state_hi.astype(F32)).astype(BF16)

    def mix(which):
        start = pl.multiple_of(which * half, half)
        at = pl.ds(start, half)
        position = z * tokens + start + 1 + lax.broadcasted_iota(jnp.int32, (half, 1), 0)
        scale = 1.0 / (position.astype(F32) * jnp.sqrt(F32(HD)))
        mixed = []
        for h in range(heads):
            cols = slice(h * HD, (h + 1) * HD)
            q = projected[at, cols]
            carried = dot(q, state_hi[cols]) + dot(q, state_lo[cols])
            mixed.append(((inside[at, cols] + carried) * scale).astype(BF16))
        return jnp.concatenate(mixed, axis=1)

    mixed_out[...] = mix(other)
    mixed_copy = core_copy(mixed_out, mixed_in, 0)
    mixed_copy.start()
    far_copies[2].start()
    own_at = pl.ds(pl.multiple_of(head * half, half), half)
    residual[...] = dot(mix(head), out_weight[...]) + series[own_at, :].astype(F32)
    out_copy.wait_recv()
    mixed_copy.wait_recv()
    total = residual[...] + dot(mixed_in[...], out_far[...])
    residual[...] = total
    normed_moe = rms_scale(total, norm_moe[...][None]).astype(BF16)
    send_rows[...] = dot(placing[...], normed_moe).astype(BF16)

    def row_copy(to_z, to_y):
        to = to_z * dp_n + to_y
        return pltpu.make_async_remote_copy(
            src_ref=send_rows.at[slab(to)],
            dst_ref=recv_rows.at[slab(me)],
            send_sem=d_send.at[to],
            recv_sem=d_recv.at[me],
            device_id={"seq": to_z, "dp": to_y},
            device_id_type=MESH,
        )

    def row_arrival(from_z, from_y):
        source = from_z * dp_n + from_y
        return pltpu.make_async_remote_copy(
            src_ref=send_rows.at[slab(source)],
            dst_ref=recv_rows.at[slab(source)],
            send_sem=d_send.at[source],
            recv_sem=d_recv.at[source],
            device_id={"seq": from_z, "dp": from_y},
            device_id_type=MESH,
        )

    def back_copy(to_z, to_y):
        to = to_z * dp_n + to_y
        return pltpu.make_async_remote_copy(
            src_ref=out_rows.at[slab(to)],
            dst_ref=back_rows.at[slab(me)],
            send_sem=b_send.at[to],
            recv_sem=b_recv.at[me],
            device_id={"seq": to_z, "dp": to_y},
            device_id_type=MESH,
        )

    def back_arrival(from_z, from_y):
        source = from_z * dp_n + from_y
        return pltpu.make_async_remote_copy(
            src_ref=out_rows.at[slab(source)],
            dst_ref=back_rows.at[slab(source)],
            send_sem=b_send.at[source],
            recv_sem=b_recv.at[source],
            device_id={"seq": from_z, "dp": from_y},
            device_id_type=MESH,
        )

    def dispatch(i):
        for j in range(2):
            for_peers(2 * i + j, 1, lambda a, b: row_copy(a, b).start())

    dispatch(0)
    recv_rows[slab(me), :] = send_rows[slab(me), :]

    logits = dot(normed_moe, router_weight[...], ((1,), (1,)))
    gate_value = jax.nn.sigmoid(jnp.sum(logits * picked, axis=1, keepdims=True))

    for copy in own_copies:
        copy.wait()
    for copy in far_copies:
        copy.wait()

    group = dp_n * cap
    units = gate_v.shape[2]
    tile = units // 3

    def expert_group(i, carry):
        @pl.when(i % 2 == 1)
        def _():
            for j in range(2):
                for_peers(i - 1 + j, 1, lambda a, b: row_copy(a, b).wait_send())

            @pl.when(i + 1 < seq_n)
            def _():
                dispatch((i + 1) // 2)

        source_z = for_peers(i, -1, lambda a, b: row_arrival(a, b).wait_recv())
        at = pl.ds(pl.multiple_of(source_z * group, group), group)
        x = recv_rows[at, :]
        for side in range(2):
            for c in range(units // tile):
                cols = slice(c * tile, (c + 1) * tile)
                g = dot(x, gate_v[side, :, cols])
                u = dot(x, up_v[side, :, cols])
                hidden[:, side * units + c * tile : side * units + (c + 1) * tile] = (
                    g * jax.nn.sigmoid(g) * u
                ).astype(BF16)
        out = dot(hidden[:, :units], down_v[0]) + dot(hidden[:, units:], down_v[1])
        out_rows[at, :] = out.astype(BF16)
        for_peers(i, -1, lambda a, b: back_copy(a, b).start())
        return carry

    lax.fori_loop(0, seq_n, expert_group, 0)
    back_rows[slab(me), :] = out_rows[slab(me), :]

    def await_back(i, carry):
        for_peers(i, 1, lambda a, b: back_arrival(a, b).wait_recv())
        return carry

    lax.fori_loop(0, seq_n, await_back, 0)
    routed = dot(routing[...], back_rows[...])
    layer_out[...] = (residual[...] + gate_value * routed).astype(BF16)

    def sent_rows(i, carry):
        for_peers(i, -1, lambda a, b: back_copy(a, b).wait_send())
        return carry

    lax.fori_loop(0, seq_n, sent_rows, 0)

    def sent_state(j, carry):
        state_copy(seq_n - 1 - j).wait_send()
        return carry

    lax.fori_loop(0, seq_n - 1 - z, sent_state, 0)
    mixed_copy.wait_send()
    out_copy.wait_send()


def on_device(
    series,
    norm_attn,
    qkv_weight,
    out_weight,
    norm_moe,
    router_weight,
    expert_ids,
    gate_weight,
    up_weight,
    down_weight,
):
    seq_n, head_n, dp_n = lax.axis_size("seq"), lax.axis_size("head"), lax.axis_size("dp")
    tokens, width = series.shape[1:]
    assert head_n == 2 and tokens == BLOCK and seq_n % 2 == 0
    rows = tokens // 2
    experts = router_weight.shape[1]
    peers = seq_n * dp_n
    assert experts == peers
    local = qkv_weight.shape[2]
    units = gate_weight.shape[2]
    capacity = 2 * rows // experts
    cap = -(-capacity // 16) * 16
    slots = experts * cap
    vmem = pl.BlockSpec(memory_space=pltpu.VMEM)
    hbm = pl.BlockSpec(memory_space=pltpu.HBM)
    dma = pltpu.SemaphoreType.DMA
    out = pl.pallas_call(
        functools.partial(layer_kernel, seq_n, dp_n, cap),
        out_shape=jax.ShapeDtypeStruct((rows, width), BF16),
        in_specs=[hbm] * 10,
        out_specs=vmem,
        scratch_shapes=[
            pltpu.VMEM((tokens, width), BF16),
            pltpu.VMEM((width,), F32),
            pltpu.VMEM((3, width, local), BF16),
            pltpu.VMEM((local, width), BF16),
            pltpu.VMEM((width,), F32),
            pltpu.VMEM((experts, width), BF16),
            pltpu.VMEM((1, rows), jnp.int32),
            pltpu.VMEM((2, width, units), BF16),
            pltpu.VMEM((2, width, units), BF16),
            pltpu.VMEM((2, units, width), BF16),
            pltpu.VMEM((tokens, width), BF16),
            pltpu.VMEM((tokens, 3 * local), BF16),
            pltpu.VMEM((local, HD), BF16),
            pltpu.VMEM((seq_n, local, HD), BF16),
            pltpu.VMEM((local, HD), F32),
            pltpu.VMEM((tokens, local), F32),
            pltpu.VMEM((rows, local), BF16),
            pltpu.VMEM((rows, local), BF16),
            pltpu.VMEM((local, width), BF16),
            pltpu.VMEM((rows, width), F32),
            pltpu.VMEM((rows, slots), BF16),
            pltpu.VMEM((slots, rows), BF16),
            pltpu.VMEM((dp_n * cap, 2 * units), BF16),
            pltpu.VMEM((slots, width), BF16),
            pltpu.VMEM((slots, width), BF16),
            pltpu.VMEM((slots, width), BF16),
            pltpu.VMEM((slots, width), BF16),
            dma((9,)),
            dma((3,)),
            dma((3,)),
            dma((3,)),
            dma((seq_n,)),
            dma((seq_n,)),
            dma((2,)),
            dma((2,)),
            dma((peers,)),
            dma((peers,)),
            dma((peers,)),
            dma((peers,)),
        ],
        compiler_params=pltpu.CompilerParams(
            collective_id=0, has_side_effects=True, vmem_limit_bytes=44 * 1024 * 1024
        ),
        name="layer",
    )(
        *[
            pltpu.with_memory_space_constraint(operand, pltpu.HBM)
            for operand in (
                series[0],
                norm_attn,
                jnp.transpose(qkv_weight, (1, 0, 2)),
                out_weight,
                norm_moe,
                router_weight.T,
                expert_ids.reshape(1, rows),
                gate_weight,
                up_weight,
                down_weight,
            )
        ]
    )
    return out[None]


def solution(mesh):
    in_specs = (
        P("dp", "seq", None),
        P(),
        P(None, None, "head"),
        P("head", None),
        P(),
        P(),
        P("dp", ("seq", "head"), None),
        P(("seq", "dp"), None, "head"),
        P(("seq", "dp"), None, "head"),
        P(("seq", "dp"), "head", None),
    )
    out_specs = P("dp", ("seq", "head"), None)
    return jax.shard_map(
        on_device, mesh=mesh, in_specs=in_specs, out_specs=out_specs, check_vma=False
    )
```

```python
import functools

import jax
import jax.numpy as jnp
from jax import lax
from jax.experimental import pallas as pl
from jax.experimental.pallas import tpu as pltpu
from jax.sharding import PartitionSpec as P

HD = 128
BLOCK = 512
NORM_EPS = 1e-06
MESH = pl.DeviceIdType.MESH
F32 = jnp.float32
BF16 = jnp.bfloat16


def rms_scale(values, gain):
    return values * lax.rsqrt(jnp.mean(values * values, axis=-1, keepdims=True) + NORM_EPS) * gain


def dot(a, b, dims=((1,), (0,))):
    return lax.dot_general(a, b, (dims, ((), ())), preferred_element_type=F32)


def layer_kernel(
    seq_n,
    dp_n,
    cap,
    series_hbm,
    norm_attn_hbm,
    qkv_hbm,
    out_hbm,
    norm_moe_hbm,
    router_hbm,
    ids_hbm,
    gate_hbm,
    up_hbm,
    down_hbm,
    layer_out,
    series,
    norm_attn,
    qkv_weight,
    out_weight,
    norm_moe,
    router_weight,
    expert_ids,
    gate_v,
    up_v,
    down_v,
    normed,
    projected,
    state_sum,
    state_own,
    state_in,
    before,
    inside,
    mixed_out,
    mixed_in,
    out_far,
    residual,
    routing,
    placing,
    hidden,
    send_rows,
    recv_rows,
    out_rows,
    back_rows,
    in_sem,
    own_sem,
    w_send,
    w_recv,
    s_send,
    s_recv,
    r_send,
    r_recv,
    d_send,
    d_recv,
    b_send,
    b_recv,
):
    z = lax.axis_index("seq")
    head = lax.axis_index("head")
    y = lax.axis_index("dp")
    other = 1 - head
    me = z * dp_n + y
    tokens, width = series.shape
    rows = tokens // 2
    local = qkv_weight.shape[2]
    heads = local // HD
    half = rows

    def step_of(i):
        return (1 + (seq_n // 2 + i - 2 + seq_n - 1) % (seq_n - 1)) * ((i + seq_n - 1) // seq_n)

    def for_peers(i, sign, act):
        k = step_of(i)
        there = (z + sign * k + seq_n) % seq_n
        for d in range(dp_n):
            col = (y + sign * d + dp_n) % dp_n
            if d == 0:
                @pl.when(k != 0)
                def _():
                    act(there, col)
            else:
                act(there, col)
        return there

    def slab(expert):
        return pl.ds(pl.multiple_of(expert * cap, cap), cap)

    fetches = [
        pltpu.make_async_copy(src, dst, in_sem.at[j])
        for j, (src, dst) in enumerate(
            (
                (series_hbm, series),
                (norm_attn_hbm, norm_attn),
                (qkv_hbm.at[1], qkv_weight.at[1]),
                (qkv_hbm.at[2], qkv_weight.at[2]),
                (qkv_hbm.at[0], qkv_weight.at[0]),
                (ids_hbm, expert_ids),
                (out_hbm, out_weight),
                (norm_moe_hbm, norm_moe),
                (router_hbm, router_weight),
            )
        )
    ]
    for fetch in fetches:
        fetch.start()

    barrier = pltpu.get_barrier_semaphore()
    pl.semaphore_signal(barrier, inc=1, device_id={"head": other}, device_id_type=MESH)

    def greet(i, carry):
        for_peers(
            i,
            1,
            lambda a, b: pl.semaphore_signal(
                barrier, inc=1, device_id={"seq": a, "dp": b}, device_id_type=MESH
            ),
        )
        return carry

    lax.fori_loop(0, seq_n, greet, 0)

    def core_copy(src, dst, j):
        return pltpu.make_async_remote_copy(
            src_ref=src,
            dst_ref=dst,
            send_sem=r_send.at[j],
            recv_sem=r_recv.at[j],
            device_id={"head": other},
            device_id_type=MESH,
        )

    weights = ((gate_hbm, gate_v), (up_hbm, up_v), (down_hbm, down_v))
    own_copies = [
        pltpu.make_async_copy(src.at[0], dst.at[0], own_sem.at[j])
        for j, (src, dst) in enumerate(weights)
    ]
    far_copies = [
        pltpu.make_async_remote_copy(
            src_ref=src.at[0],
            dst_ref=dst.at[1],
            send_sem=w_send.at[j],
            recv_sem=w_recv.at[j],
            device_id={"head": other},
            device_id_type=MESH,
        )
        for j, (src, dst) in enumerate(weights)
    ]
    fetches[0].wait()
    fetches[1].wait()
    normed[...] = rms_scale(series[...].astype(F32), norm_attn[...][None]).astype(BF16)
    for j in (1, 2):
        fetches[1 + j].wait()
        projected[:, j * local : (j + 1) * local] = dot(normed[...], qkv_weight[j]).astype(BF16)
    for h in range(heads):
        at = pl.ds(h * HD, HD)
        keys = projected[:, local + h * HD : local + (h + 1) * HD]
        values = projected[:, 2 * local + h * HD : 2 * local + (h + 1) * HD]
        state_sum[at, :] = dot(keys, values, ((0,), (0,)))

    pl.semaphore_wait(barrier, seq_n * dp_n)

    def state_copy(source, to, h):
        at = pl.ds(h * HD, HD)
        return pltpu.make_async_remote_copy(
            src_ref=state_own.at[at],
            dst_ref=state_in.at[source, at],
            send_sem=s_send.at[to, h],
            recv_sem=s_recv.at[source, h],
            device_id={"seq": to},
            device_id_type=MESH,
        )

    odd = z % 2

    @pl.when(odd == 0)
    def _():
        state_own[...] = state_sum[...].astype(BF16)
        for h in range(heads):
            state_copy(z, z + 1, h).start()

    for fetch in fetches[4:]:
        fetch.wait()
    out_copy = core_copy(out_weight, out_far, 1)
    out_copy.start()
    for copy in own_copies:
        copy.start()
    far_copies[0].start()
    far_copies[1].start()

    projected[:, :local] = dot(normed[...], qkv_weight[0]).astype(BF16)

    @pl.when(odd == 1)
    def _():
        for h in range(heads):
            at = pl.ds(h * HD, HD)
            state_copy(z - 1, z - 1, h).wait_recv()
            pair = state_sum[at, :] + state_in[z - 1, at, :].astype(F32)
            state_own[at, :] = pair.astype(BF16)

            def send_pair(j, carry):
                state_copy(z, seq_n - 1 - j, h).start()
                return carry

            lax.fori_loop(0, seq_n - 1 - z, send_pair, 0)

    for h in range(heads):
        cols = slice(h * HD, (h + 1) * HD)
        for part in range(2):
            low, high = part * half, (part + 1) * half
            q = projected[low:high, cols]
            keys = projected[:high, local + h * HD : local + (h + 1) * HD]
            values = projected[:high, 2 * local + h * HD : 2 * local + (h + 1) * HD]
            scores = dot(q, keys, ((1,), (1,)))
            t = lax.broadcasted_iota(jnp.int32, scores.shape, 0) + low
            s = lax.broadcasted_iota(jnp.int32, scores.shape, 1)
            scores = jnp.where(t >= s, scores, 0.0).astype(BF16)
            inside[low:high, cols] = dot(scores, values)

    ids = expert_ids[...]
    experts = router_weight.shape[0]
    slots = routing.shape[1]
    picked_row = (ids == lax.broadcasted_iota(jnp.int32, (experts, rows), 0)).astype(F32)
    earlier = lax.broadcasted_iota(jnp.int32, (rows, rows), 0) < lax.broadcasted_iota(
        jnp.int32, (rows, rows), 1
    )
    ranks = dot(picked_row.astype(BF16), earlier.astype(F32).astype(BF16))
    rank = jnp.sum(ranks * picked_row, axis=0, keepdims=True)
    slot = ids * cap + rank.astype(jnp.int32)
    placing[...] = (
        (slot == lax.broadcasted_iota(jnp.int32, (slots, rows), 0)).astype(F32).astype(BF16)
    )
    columns = jnp.transpose(jnp.broadcast_to(slot.astype(F32), (HD, rows)))
    slot_column = columns[:, :1].astype(jnp.int32)
    routing[...] = (
        (slot_column == lax.broadcasted_iota(jnp.int32, (rows, slots), 1)).astype(F32).astype(BF16)
    )
    picked = (
        slot_column // cap == lax.broadcasted_iota(jnp.int32, (rows, experts), 1)
    ).astype(F32)

    before[...] = jnp.zeros_like(before)

    @pl.when(odd == 1)
    def _():
        before[...] = state_in[z - 1].astype(F32)

    def add_pair(j, carry):
        source = 2 * j + 1
        for h in range(heads):
            state_copy(source, source, h).wait_recv()
        before[...] += state_in[source].astype(F32)
        return carry

    lax.fori_loop(0, z // 2, add_pair, 0)

    state_hi = before[...].astype(BF16)
    state_lo = (before[...] - state_hi.astype(F32)).astype(BF16)

    def mix(which):
        start = pl.multiple_of(which * half, half)
        at = pl.ds(start, half)
        position = z * tokens + start + 1 + lax.broadcasted_iota(jnp.int32, (half, 1), 0)
        scale = 1.0 / (position.astype(F32) * jnp.sqrt(F32(HD)))
        mixed = []
        for h in range(heads):
            cols = slice(h * HD, (h + 1) * HD)
            q = projected[at, cols]
            carried = dot(q, state_hi[cols]) + dot(q, state_lo[cols])
            mixed.append(((inside[at, cols] + carried) * scale).astype(BF16))
        return jnp.concatenate(mixed, axis=1)

    mixed_out[...] = mix(other)
    mixed_copy = core_copy(mixed_out, mixed_in, 0)
    mixed_copy.start()
    far_copies[2].start()
    own_at = pl.ds(pl.multiple_of(head * half, half), half)
    residual[...] = dot(mix(head), out_weight[...]) + series[own_at, :].astype(F32)
    out_copy.wait_recv()
    mixed_copy.wait_recv()
    total = residual[...] + dot(mixed_in[...], out_far[...])
    residual[...] = total
    normed_moe = rms_scale(total, norm_moe[...][None]).astype(BF16)
    send_rows[...] = dot(placing[...], normed_moe).astype(BF16)

    def row_copy(to_z, to_y):
        to = to_z * dp_n + to_y
        return pltpu.make_async_remote_copy(
            src_ref=send_rows.at[slab(to)],
            dst_ref=recv_rows.at[slab(me)],
            send_sem=d_send.at[to],
            recv_sem=d_recv.at[me],
            device_id={"seq": to_z, "dp": to_y},
            device_id_type=MESH,
        )

    def row_arrival(from_z, from_y):
        source = from_z * dp_n + from_y
        return pltpu.make_async_remote_copy(
            src_ref=send_rows.at[slab(source)],
            dst_ref=recv_rows.at[slab(source)],
            send_sem=d_send.at[source],
            recv_sem=d_recv.at[source],
            device_id={"seq": from_z, "dp": from_y},
            device_id_type=MESH,
        )

    def back_copy(to_z, to_y):
        to = to_z * dp_n + to_y
        return pltpu.make_async_remote_copy(
            src_ref=out_rows.at[slab(to)],
            dst_ref=back_rows.at[slab(me)],
            send_sem=b_send.at[to],
            recv_sem=b_recv.at[me],
            device_id={"seq": to_z, "dp": to_y},
            device_id_type=MESH,
        )

    def back_arrival(from_z, from_y):
        source = from_z * dp_n + from_y
        return pltpu.make_async_remote_copy(
            src_ref=out_rows.at[slab(source)],
            dst_ref=back_rows.at[slab(source)],
            send_sem=b_send.at[source],
            recv_sem=b_recv.at[source],
            device_id={"seq": from_z, "dp": from_y},
            device_id_type=MESH,
        )

    def dispatch(i):
        for j in range(2):
            for_peers(2 * i + j, 1, lambda a, b: row_copy(a, b).start())

    dispatch(0)
    recv_rows[slab(me), :] = send_rows[slab(me), :]

    logits = dot(normed_moe, router_weight[...], ((1,), (1,)))
    gate_value = jax.nn.sigmoid(jnp.sum(logits * picked, axis=1, keepdims=True))

    for copy in own_copies:
        copy.wait()
    for copy in far_copies:
        copy.wait()

    group = dp_n * cap
    units = gate_v.shape[2]
    tile = units // 3

    def expert_groups(i, carry):
        for j in range(2):
            for_peers(2 * i + j, 1, lambda a, b: row_copy(a, b).wait_send())

        @pl.when(i + 1 < seq_n // 2)
        def _():
            dispatch(i + 1)

        places = []
        for j in range(2):
            source_z = for_peers(2 * i + j, -1, lambda a, b: row_arrival(a, b).wait_recv())
            places.append(pl.ds(pl.multiple_of(source_z * group, group), group))
        x = jnp.concatenate([recv_rows[at, :] for at in places], axis=0)
        for side in range(2):
            for c in range(units // tile):
                cols = slice(c * tile, (c + 1) * tile)
                g = dot(x, gate_v[side, :, cols])
                u = dot(x, up_v[side, :, cols])
                hidden[:, side * units + c * tile : side * units + (c + 1) * tile] = (
                    g * jax.nn.sigmoid(g) * u
                ).astype(BF16)
        out = dot(hidden[:, :units], down_v[0]) + dot(hidden[:, units:], down_v[1])
        for j, at in enumerate(places):
            out_rows[at, :] = out[j * group : (j + 1) * group].astype(BF16)
            for_peers(2 * i + j, -1, lambda a, b: back_copy(a, b).start())
        return carry

    lax.fori_loop(0, seq_n // 2, expert_groups, 0)
    back_rows[slab(me), :] = out_rows[slab(me), :]

    def await_back(i, carry):
        for_peers(i, 1, lambda a, b: back_arrival(a, b).wait_recv())
        return carry

    lax.fori_loop(0, seq_n, await_back, 0)
    routed = dot(routing[...], back_rows[...])
    layer_out[...] = (residual[...] + gate_value * routed).astype(BF16)

    def sent_rows(i, carry):
        for_peers(i, -1, lambda a, b: back_copy(a, b).wait_send())
        return carry

    lax.fori_loop(0, seq_n, sent_rows, 0)

    @pl.when(odd == 0)
    def _():
        for h in range(heads):
            state_copy(z, z + 1, h).wait_send()

    @pl.when(odd == 1)
    def _():
        def sent_pair(j, carry):
            for h in range(heads):
                state_copy(z, seq_n - 1 - j, h).wait_send()
            return carry

        lax.fori_loop(0, seq_n - 1 - z, sent_pair, 0)

    mixed_copy.wait_send()
    out_copy.wait_send()


def on_device(
    series,
    norm_attn,
    qkv_weight,
    out_weight,
    norm_moe,
    router_weight,
    expert_ids,
    gate_weight,
    up_weight,
    down_weight,
):
    seq_n, head_n, dp_n = lax.axis_size("seq"), lax.axis_size("head"), lax.axis_size("dp")
    tokens, width = series.shape[1:]
    assert head_n == 2 and tokens == BLOCK and seq_n % 2 == 0
    rows = tokens // 2
    experts = router_weight.shape[1]
    peers = seq_n * dp_n
    assert experts == peers
    local = qkv_weight.shape[2]
    units = gate_weight.shape[2]
    capacity = 2 * rows // experts
    cap = -(-capacity // 16) * 16
    slots = experts * cap
    vmem = pl.BlockSpec(memory_space=pltpu.VMEM)
    hbm = pl.BlockSpec(memory_space=pltpu.HBM)
    dma = pltpu.SemaphoreType.DMA
    out = pl.pallas_call(
        functools.partial(layer_kernel, seq_n, dp_n, cap),
        out_shape=jax.ShapeDtypeStruct((rows, width), BF16),
        in_specs=[hbm] * 10,
        out_specs=vmem,
        scratch_shapes=[
            pltpu.VMEM((tokens, width), BF16),
            pltpu.VMEM((width,), F32),
            pltpu.VMEM((3, width, local), BF16),
            pltpu.VMEM((local, width), BF16),
            pltpu.VMEM((width,), F32),
            pltpu.VMEM((experts, width), BF16),
            pltpu.VMEM((1, rows), jnp.int32),
            pltpu.VMEM((2, width, units), BF16),
            pltpu.VMEM((2, width, units), BF16),
            pltpu.VMEM((2, units, width), BF16),
            pltpu.VMEM((tokens, width), BF16),
            pltpu.VMEM((tokens, 3 * local), BF16),
            pltpu.VMEM((local, HD), F32),
            pltpu.VMEM((local, HD), BF16),
            pltpu.VMEM((seq_n, local, HD), BF16),
            pltpu.VMEM((local, HD), F32),
            pltpu.VMEM((tokens, local), F32),
            pltpu.VMEM((rows, local), BF16),
            pltpu.VMEM((rows, local), BF16),
            pltpu.VMEM((local, width), BF16),
            pltpu.VMEM((rows, width), F32),
            pltpu.VMEM((rows, slots), BF16),
            pltpu.VMEM((slots, rows), BF16),
            pltpu.VMEM((2 * dp_n * cap, 2 * units), BF16),
            pltpu.VMEM((slots, width), BF16),
            pltpu.VMEM((slots, width), BF16),
            pltpu.VMEM((slots, width), BF16),
            pltpu.VMEM((slots, width), BF16),
            dma((9,)),
            dma((3,)),
            dma((3,)),
            dma((3,)),
            dma((seq_n, local // HD)),
            dma((seq_n, local // HD)),
            dma((2,)),
            dma((2,)),
            dma((peers,)),
            dma((peers,)),
            dma((peers,)),
            dma((peers,)),
        ],
        compiler_params=pltpu.CompilerParams(
            collective_id=0, has_side_effects=True, vmem_limit_bytes=44 * 1024 * 1024
        ),
        name="layer",
    )(
        *[
            pltpu.with_memory_space_constraint(operand, pltpu.HBM)
            for operand in (
                series[0],
                norm_attn,
                jnp.transpose(qkv_weight, (1, 0, 2)),
                out_weight,
                norm_moe,
                router_weight.T,
                expert_ids.reshape(1, rows),
                gate_weight,
                up_weight,
                down_weight,
            )
        ]
    )
    return out[None]


def solution(mesh):
    in_specs = (
        P("dp", "seq", None),
        P(),
        P(None, None, "head"),
        P("head", None),
        P(),
        P(),
        P("dp", ("seq", "head"), None),
        P(("seq", "dp"), None, "head"),
        P(("seq", "dp"), None, "head"),
        P(("seq", "dp"), "head", None),
    )
    out_specs = P("dp", ("seq", "head"), None)
    return jax.shard_map(
        on_device, mesh=mesh, in_specs=in_specs, out_specs=out_specs, check_vma=False
    )
```
